128 devices in a mesh: row: 16 (over z, x), col: 8 (over y, core).
Axes of the slice: x: 4, y: 4, z: 4, core: 2. Of those that a mesh axis runs over, the one named last changes fastest.
Arguments:
- right_side: float32 [64, 1024, 256], P('row', 'col'), may hold values from -12 to 12
- permeability: bfloat16 [64, 1024, 256], P('row', 'col'), may hold values from 0.25 to 4
- lift_weight: float32 [16, 3], replicated, may hold values from -3 to 3
- spectral_weight: float32 [2, 32, 16, 16, 512], P(None, 'row', None, None, 'col'), may hold values from -3 to 3
- mix_weight: float32 [16, 17], replicated, may hold values from -3 to 3
- proj_weight: float32 [17], replicated, may hold values from -3 to 3
Outputs:
- solution: float32 [64, 1024, 256], P('row', 'col')
- residual: float32 [64, 1024, 256], P('row', 'col')
- kept: float32 [2, 64, 1024, 256], P(None, 'row', 'col')
The draws below stay inside these ranges and needn't reach their ends.
All inputs are finite; a program needn't handle non-finite values.
Results may differ from the reference program's by a relative error of at most 0.0007.
Values may be sent and summed in bfloat16 or wider, within the bound.
A program may use at most 128 MiB of HBM per device.

```python
import math
import jax
import jax.numpy as jnp
from jax import lax

NZ = 256
CHANNELS = 16
KX = 16
KY = 32
KZ = 32
ITERS = 2
NX = 64
NY = 1024


def draw_right_side(key, part):
    first_frac = lax.broadcasted_iota(jnp.float32, (NX, NY, NZ), 0) / NX
    second_frac = lax.broadcasted_iota(jnp.float32, (NX, NY, NZ), 1) / NY
    ramp = 0.6 + 0.8 * first_frac + 0.6 * second_frac
    noise = jnp.clip(jax.random.normal(key, (NX, NY, NZ), jnp.float32), -6.0, 6.0)
    return noise * ramp


def steps_of(key, dims, shards, least, largest):
    factor_of = 1.0
    for dim, shards_of in shards:
        draws = jax.random.uniform(jax.random.fold_in(jax.random.fold_in(key, 6), dim), (shards_of,), jnp.float32, least / len(shards), largest / len(shards))
        factor_of = factor_of * jnp.repeat(jnp.exp(draws), dims[dim] // shards_of).reshape((-1,) + (1,) * (len(dims) - 1 - dim))
    return factor_of


def centred(rng, dims, scale, bound, shards=(), kind=jnp.bfloat16):
    drawn = jax.random.normal(rng, dims, jnp.float32) * scale
    if len(shards) > 0:
        drawn = steps_of(rng, dims, shards, -0.22, 0.18) * drawn
    return jnp.clip(drawn, min=-bound, max=bound).astype(kind)


def setup_inputs(seed: int = 0) -> dict:
    streams_of = jax.random.split(jax.random.key(seed), 7)
    return {
        "right_side": draw_right_side(jax.random.fold_in(streams_of[6], 71), 0),
        "permeability": jnp.clip(jnp.exp(math.log(4.0) - 2.7725887 * jax.random.uniform(streams_of[1], (NX, NY, NZ), jnp.float32) ** steps_of(streams_of[1], (NX, NY, NZ), ((0, 16), (1, 8)), -0.2, 0.2)), 0.25, 4.0).astype(jnp.bfloat16),
        "lift_weight": centred(streams_of[2], (CHANNELS, 3), 0.8, 3.0, (), jnp.float32),
        "spectral_weight": centred(streams_of[3], (2, KZ, CHANNELS, CHANNELS, KX * KY), 0.25, 3.0, ((1, 16), (4, 8)), jnp.float32),
        "mix_weight": centred(streams_of[4], (CHANNELS, CHANNELS + 1), 0.25, 3.0, (), jnp.float32),
        "proj_weight": centred(streams_of[5], (CHANNELS + 1,), 0.35, 3.0, (), jnp.float32),
    }


HIGHEST = lax.Precision.HIGHEST

def einsum_high(form, left, right):
    return jnp.einsum(form, left, right, precision=HIGHEST)

def harmonic(first, second):
    return 2.0 * first * second / (first + second)

def wave_table(freqs, places, length):
    turns = freqs[None, :] * places[:, None] % length
    angle = turns.astype(jnp.float32) * (2.0 * jnp.pi / length)
    return (jnp.cos(angle), jnp.sin(angle))

def signed_freqs(count):
    return jnp.arange(count, dtype=jnp.int32) - count // 2

def apply_operator(field, faces):
    first, second, third = faces
    padded = jnp.pad(field, 1)
    total = first[:-1] * (field - padded[:-2, 1:-1, 1:-1])
    total = total + first[1:] * (field - padded[2:, 1:-1, 1:-1])
    total = total + second[:, :-1] * (field - padded[1:-1, :-2, 1:-1])
    total = total + second[:, 1:] * (field - padded[1:-1, 2:, 1:-1])
    total = total + third[:, :, :-1] * (field - padded[1:-1, 1:-1, :-2])
    total = total + third[:, :, 1:] * (field - padded[1:-1, 1:-1, 2:])
    return total

def precondition(res, squares_total, log_perm, lift_weight, spectral_weight, mix_weight, proj_weight, tables):
    cosine_rows, sine_rows, cosine_cols, sine_cols, cosine_deep, sine_deep = tables
    cells = NX * NY * NZ
    scale = jnp.sqrt(squares_total / cells + 1e-06)
    scaled = res / scale

    def lifted(channel):
        return jax.nn.gelu(lift_weight[channel, 0] * scaled + lift_weight[channel, 1] * log_perm + lift_weight[channel, 2])
    real_list = []
    imag_list = []
    for channel in range(CHANNELS):
        values = lifted(channel)
        deep_real = einsum_high('xyz,zk->xyk', values, cosine_deep)
        deep_imag = -einsum_high('xyz,zk->xyk', values, sine_deep)
        first_real = einsum_high('xyk,xf->fyk', deep_real, cosine_rows) + einsum_high('xyk,xf->fyk', deep_imag, sine_rows)
        first_imag = einsum_high('xyk,xf->fyk', deep_imag, cosine_rows) - einsum_high('xyk,xf->fyk', deep_real, sine_rows)
        second_real = einsum_high('fyk,yg->fgk', first_real, cosine_cols) + einsum_high('fyk,yg->fgk', first_imag, sine_cols)
        second_imag = einsum_high('fyk,yg->fgk', first_imag, cosine_cols) - einsum_high('fyk,yg->fgk', first_real, sine_cols)
        real_list.append(second_real)
        imag_list.append(second_imag)
    spec_real = jnp.stack(real_list)
    spec_imag = jnp.stack(imag_list)
    table = spectral_weight.reshape(2, KZ, CHANNELS, CHANNELS, KX, KY)
    mixed_real = einsum_high('cfgk,kcofg->ofgk', spec_real, table[0]) - einsum_high('cfgk,kcofg->ofgk', spec_imag, table[1])
    mixed_imag = einsum_high('cfgk,kcofg->ofgk', spec_imag, table[0]) + einsum_high('cfgk,kcofg->ofgk', spec_real, table[1])
    output = jnp.zeros_like(res)
    for target in range(CHANNELS):
        back_real = einsum_high('fgk,yg->fyk', mixed_real[target], cosine_cols) - einsum_high('fgk,yg->fyk', mixed_imag[target], sine_cols)
        back_imag = einsum_high('fgk,yg->fyk', mixed_imag[target], cosine_cols) + einsum_high('fgk,yg->fyk', mixed_real[target], sine_cols)
        whole_real = einsum_high('fyk,xf->xyk', back_real, cosine_rows) - einsum_high('fyk,xf->xyk', back_imag, sine_rows)
        whole_imag = einsum_high('fyk,xf->xyk', back_imag, cosine_rows) + einsum_high('fyk,xf->xyk', back_real, sine_rows)
        spatial = (einsum_high('xyk,zk->xyz', whole_real, cosine_deep) - einsum_high('xyk,zk->xyz', whole_imag, sine_deep)) / cells
        point = mix_weight[target, CHANNELS] + jnp.zeros_like(res)
        for channel in range(CHANNELS):
            point = point + mix_weight[target, channel] * lifted(channel)
        output = output + proj_weight[target] * jax.nn.gelu(spatial + point)
    return scale * (output + proj_weight[CHANNELS])

def reference(right_side, permeability, lift_weight, spectral_weight, mix_weight, proj_weight):
    conductance = permeability.astype(jnp.float32)
    log_perm = jnp.log(conductance)
    edged = jnp.pad(conductance, 1, mode='edge')
    faces = (harmonic(edged[:-1, 1:-1, 1:-1], edged[1:, 1:-1, 1:-1]), harmonic(edged[1:-1, :-1, 1:-1], edged[1:-1, 1:, 1:-1]), harmonic(edged[1:-1, 1:-1, :-1], edged[1:-1, 1:-1, 1:]))
    cosine_rows, sine_rows = wave_table(signed_freqs(KX), jnp.arange(NX, dtype=jnp.int32), NX)
    cosine_cols, sine_cols = wave_table(signed_freqs(KY), jnp.arange(NY, dtype=jnp.int32), NY)
    cosine_deep, sine_deep = wave_table(jnp.arange(KZ, dtype=jnp.int32), jnp.arange(NZ, dtype=jnp.int32), NZ)
    tables = (cosine_rows, sine_rows, cosine_cols, sine_cols, cosine_deep, sine_deep)

    def precond(res):
        return precondition(res, jnp.sum(res * res), log_perm, lift_weight, spectral_weight, mix_weight, proj_weight, tables)
    solution = jnp.zeros_like(right_side)
    residual = right_side
    update = precond(residual)
    kept = [update]
    direction = update
    for step in range(ITERS):
        image = apply_operator(direction, faces)
        curvature = jnp.sum(direction * image)
        alpha = jnp.sum(residual * direction) / curvature
        solution = solution + alpha * direction
        residual = residual - alpha * image
        if step + 1 < ITERS:
            update = precond(residual)
            kept.append(update)
            beta = jnp.sum(update * image) / curvature
            direction = update - beta * direction
    return (solution, residual, jnp.stack(kept))
```

```python
import jax
import jax.numpy as jnp
import ml_dtypes
import numpy as np
from jax import lax
from jax.experimental import pallas as pl
from jax.experimental.pallas import tpu as pltpu
from jax.sharding import PartitionSpec as P

F32 = jnp.float32
BF16 = jnp.bfloat16
MESH = pl.DeviceIdType.MESH
NR, NC = 16, 8
NX, NY, NZ = 64, 1024, 256
LX, LY = NX // NR, NY // NC
CH = 16
CELLS = float(NX * NY * NZ)
GELU_A = float(np.sqrt(2.0 / np.pi))


def pieces(table):
    high = table.astype(ml_dtypes.bfloat16)
    low = (table - high.astype(np.float64)).astype(ml_dtypes.bfloat16)
    return high, low


def waves(freqs, places, length):
    angle = 2.0 * np.pi * ((freqs[None, :] * places[:, None]) % length) / length
    return np.cos(angle), np.sin(angle)


def tables():
    cz, sz = waves(np.arange(32), np.arange(NZ), NZ)
    tz = np.zeros((LX, NZ, 2, 32, LX))
    ti = np.zeros((2, 32, LX, LX, NZ))
    for x in range(LX):
        tz[x, :, 0, :, x] = cz
        tz[x, :, 1, :, x] = sz
        ti[0, :, x, x, :] = cz.T
        ti[1, :, x, x, :] = -sz.T
    tz = pieces(tz.reshape(LX * NZ, 256))[0]
    ti_high, ti_low = pieces(ti.reshape(256, LX * NZ))
    ti = np.concatenate([ti_high, ti_high, ti_low], axis=0)

    yt = np.zeros((NC, 2, 32, 2, LY))
    yi = np.zeros((NC, 2, LY, 2, 32))
    for col in range(NC):
        cy, sy = waves(np.arange(-16, 16), np.arange(LY) + col * LY, NY)
        yt[col, 0, :, 0] = cy.T
        yt[col, 0, :, 1] = -sy.T
        yt[col, 1, :, 0] = -sy.T
        yt[col, 1, :, 1] = -cy.T
        yi[col, 0, :, 0] = cy
        yi[col, 0, :, 1] = -sy
        yi[col, 1, :, 0] = sy
        yi[col, 1, :, 1] = cy
    yt = np.concatenate(pieces(yt.reshape(NC, 64, 256)), axis=1)
    yi_high, yi_low = pieces(yi.reshape(NC, 256, 64))
    yi = np.concatenate([yi_high, yi_high, yi_low], axis=2)

    cx, sx = waves(np.arange(-8, 8), np.arange(NX), NX)
    cx = cx.reshape(NR, LX, NC, 2)
    sx = sx.reshape(NR, LX, NC, 2)
    xt = np.zeros((NC, 2, 2, 2, NR, 2, 2, LX))
    xi = np.zeros((NR, 2, 2, LX, NC, 2, 2, 2))
    for kz in range(2):
        forward_cos = cx.transpose(2, 3, 0, 1)
        forward_sin = sx.transpose(2, 3, 0, 1)
        xt[:, kz, :, 0, :, 0, kz, :] = forward_cos
        xt[:, kz, :, 0, :, 1, kz, :] = forward_sin
        xt[:, kz, :, 1, :, 1, kz, :] = forward_cos
        xt[:, kz, :, 1, :, 0, kz, :] = -forward_sin
        xi[:, 0, kz, :, :, kz, :, 0] = cx
        xi[:, 0, kz, :, :, kz, :, 1] = -sx
        xi[:, 1, kz, :, :, kz, :, 1] = cx
        xi[:, 1, kz, :, :, kz, :, 0] = sx
    xt = np.concatenate(pieces(xt.reshape(64, 256)), axis=0)
    xi_high, xi_low = pieces(xi.reshape(256, 64) * (0.5 / CELLS))
    xi = np.concatenate([xi_high, xi_high, xi_low], axis=1)

    fold = np.zeros((4, 4, 32, 4, 32))
    for r in range(4):
        for c in range(4):
            fold[r, c, :, r, :] = np.eye(32)
    fold = fold.reshape(512, 128)
    spread = np.ascontiguousarray(fold.T)
    gather = np.zeros((4, 4, 2, 4, 2, 16))
    for quad in range(4):
        for r in range(4):
            for ri in range(2):
                gather[quad, r, ri, r, ri, quad * 4 : quad * 4 + 4] = 1.0
    gather = gather.reshape(32, 128)
    left = np.kron(np.eye(16), np.ones((8, 1)))
    right = np.zeros((16, 16, 2, 8))
    for c in range(16):
        right[c, c] = 1.0
    right = right.reshape(16, 256)
    b16 = lambda a: a.astype(ml_dtypes.bfloat16)
    return tz, ti, yt, yi, xt, xi, b16(fold), b16(spread), b16(gather), b16(left), b16(right)


def split(value):
    high = value.astype(BF16)
    return high, (value - high.astype(F32)).astype(BF16)


def dot(left, right):
    return jnp.dot(left, right, preferred_element_type=F32)


def kernel(
    rs, perm, lw, mw, pw, mixv, weight,
    tz, ti, yt_all, yi_all, xt, xi, fold, spread, gather, left_map, right_map,
    sol, res, kept,
    lift, point, logp, padk, padp, faces, prev, image, fresh, maps, yt, yi,
    plx, phx, ply, phy,
    sf, vf, sx, vx, sm, vm, sh, vh, modes,
    asrc, acol, bsrc, arow, state,
    perm_s, perm_r, halo_s, halo_r, f_s, f_r, x_s, x_r, m_s, m_r, h_s, h_r, ac_s, ac_r, ar_s, ar_r, table_s,
):
    row = lax.axis_index("row")
    col = lax.axis_index("col")
    up_row, down_row = lax.rem(row + 1, NR), lax.rem(row + NR - 1, NR)
    up_col, down_col = lax.rem(col + 1, NC), lax.rem(col + NC - 1, NC)

    def send(src, dst, s, r, to_row, to_col):
        return pltpu.make_async_remote_copy(
            src_ref=src, dst_ref=dst, send_sem=s, recv_sem=r, device_id=(to_row, to_col), device_id_type=MESH
        )

    table_copies = [
        pltpu.make_async_copy(yt_all.at[col], yt, table_s.at[0]),
        pltpu.make_async_copy(yi_all.at[col], yi, table_s.at[1]),
    ]
    for copy in table_copies:
        copy.start()

    barrier = pltpu.get_barrier_semaphore()

    def greet_row(k, carry):
        pl.semaphore_signal(barrier, 1, device_id=(lax.rem(row + k, NR), col), device_id_type=MESH)
        return carry

    def greet_col(k, carry):
        pl.semaphore_signal(barrier, 1, device_id=(row, lax.rem(col + k, NC)), device_id_type=MESH)
        return carry

    lax.fori_loop(1, NR, greet_row, 0)
    lax.fori_loop(1, NC, greet_col, 0)
    pl.semaphore_wait(barrier, NR + NC - 2)

    perm_copies = [
        send(perm.at[LX - 1], plx, perm_s.at[0], perm_r.at[0], up_row, col),
        send(perm.at[0], phx, perm_s.at[1], perm_r.at[1], down_row, col),
        send(perm.at[:, pl.ds(LY - 16, 16), :], ply, perm_s.at[2], perm_r.at[2], row, up_col),
        send(perm.at[:, pl.ds(0, 16), :], phy, perm_s.at[3], perm_r.at[3], row, down_col),
    ]
    for copy in perm_copies:
        copy.start()

    def sums_begin(u, tile):
        asrc[u] = tile
        acol[u, col] = tile

        def step(k, carry):
            send(asrc.at[u], acol.at[u, col], ac_s.at[u], ac_r.at[u], row, lax.rem(col + k, NC)).start()
            return carry

        lax.fori_loop(1, NC, step, 0)

    def sums_end(u):
        whole = send(acol.at[u, pl.ds(0, NC - 1)], acol.at[u, pl.ds(0, NC - 1)], ac_s.at[u], ac_r.at[u], row, col)
        whole.wait_recv()
        whole.wait_send()
        tile = jnp.sum(acol[u], axis=0)
        bsrc[u] = tile
        arow[u, row] = tile

        def step(k, carry):
            send(bsrc.at[u], arow.at[u, row], ar_s.at[u], ar_r.at[u], lax.rem(row + k, NR), col).start()
            return carry

        lax.fori_loop(1, NR, step, 0)
        whole = send(arow.at[u, pl.ds(0, NR - 1)], arow.at[u, pl.ds(0, NR - 1)], ar_s.at[u], ar_r.at[u], row, col)
        whole.wait_recv()
        whole.wait_send()
        return jnp.sum(jnp.sum(arow[u], axis=0), axis=1, keepdims=True)

    def tile_of(parts):
        rows = []
        for part in parts:
            line = jnp.sum(part, axis=0, keepdims=True)
            rows.append(line[:, :128] + line[:, 128:])
        index = lax.broadcasted_iota(jnp.int32, (8, 128), 0)
        tile = jnp.zeros((8, 128), F32)
        for i, line in enumerate(rows):
            tile = jnp.where(index == i, jnp.broadcast_to(line, (8, 128)), tile)
        return tile

    def first_pass(b, total):
        x, y = lax.div(b, 4), pl.multiple_of(lax.rem(b, 4) * 32, 32)
        value = rs[x, pl.ds(y, 32), :]
        res[x, pl.ds(y, 32), :] = value
        squares = value * value
        return total + (squares[0:8] + squares[8:16]) + (squares[16:24] + squares[24:32])

    total = lax.fori_loop(0, 16, first_pass, jnp.zeros((8, NZ), F32))
    sums_begin(0, tile_of([total]))

    def second_pass(b, carry):
        x, y = lax.div(b, 4), pl.multiple_of(lax.rem(b, 4) * 32, 32)
        value = perm[x, pl.ds(y, 32), :].astype(F32)
        padp[x + 1, pl.ds(pl.multiple_of(y + 8, 8), 32), :] = value
        logp[x, pl.ds(y, 32), :] = jnp.log(value)
        zero = jnp.zeros((32, NZ), F32)
        sol[x, pl.ds(y, 32), :] = zero
        prev[x, pl.ds(y, 32), :] = zero
        image[x, pl.ds(y, 32), :] = zero
        return carry

    lax.fori_loop(0, 16, second_pass, 0)
    mix_high, mix_low = split(mixv[:, 0:CH] * 0.5)
    rows_iota = lax.broadcasted_iota(jnp.int32, (128, 256), 0)
    lane_iota = lax.broadcasted_iota(jnp.int32, (128, 256), 1)
    same = lax.rem(rows_iota, 8) == lax.rem(lane_iota, 8)
    for n, piece in enumerate((mix_high, mix_low)):
        wide = dot(left_map[...], dot(piece, right_map[...]).astype(BF16))
        maps[n * 128 : (n + 1) * 128, :] = jnp.where(same, wide, 0.0).astype(BF16)

    for copy in perm_copies:
        copy.wait()
    padp[0, pl.ds(8, LY), :] = plx[...].astype(F32)
    padp[LX + 1, pl.ds(8, LY), :] = phx[...].astype(F32)
    for x in range(LX):
        padp[x + 1, pl.ds(0, 8), :] = ply[x].astype(F32)[8:16]
        padp[x + 1, pl.ds(LY + 8, 8), :] = phy[x].astype(F32)[0:8]

    @pl.when(row == 0)
    def _():
        padp[0, pl.ds(8, LY), :] = padp[1, pl.ds(8, LY), :]

    @pl.when(row == NR - 1)
    def _():
        padp[LX + 1, pl.ds(8, LY), :] = padp[LX, pl.ds(8, LY), :]

    @pl.when(col == 0)
    def _():
        for x in range(LX):
            padp[x + 1, pl.ds(0, 8), :] = jnp.broadcast_to(padp[x + 1, pl.ds(8, 8), :][0:1], (8, NZ))

    @pl.when(col == NC - 1)
    def _():
        for x in range(LX):
            padp[x + 1, pl.ds(LY + 8, 8), :] = jnp.broadcast_to(padp[x + 1, pl.ds(LY, 8), :][7:8], (8, NZ))

    lanes = lax.broadcasted_iota(jnp.int32, (32, NZ), 1)

    def around(ref, x, y, edge):
        own = ref[x + 1, pl.ds(y, 48), :]
        here = own[8:40]
        before = pltpu.roll(here, 1, 1)
        after = pltpu.roll(here, NZ - 1, 1)
        if edge:
            before = jnp.where(lanes == 0, here, before)
            after = jnp.where(lanes == NZ - 1, here, after)
        else:
            before = jnp.where(lanes == 0, 0.0, before)
            after = jnp.where(lanes == NZ - 1, 0.0, after)
        return here, (
            ref[x, pl.ds(pl.multiple_of(y + 8, 8), 32), :], ref[x + 2, pl.ds(pl.multiple_of(y + 8, 8), 32), :], own[7:39], own[9:41], before, after
        )

    def face_pass(b, carry):
        x, y = lax.div(b, 4), pl.multiple_of(lax.rem(b, 4) * 32, 32)
        here, others = around(padp, x, y, True)
        for n, other in enumerate(others):
            faces[n, x, pl.ds(y, 32), :] = 2.0 * here * other / (here + other)
        return carry

    lax.fori_loop(0, 16, face_pass, 0)

    for copy in table_copies:
        copy.wait()
    state[0] = jnp.broadcast_to(sums_end(0)[0:1], (8, 128))
    state[1] = jnp.ones((8, 128), F32)

    mask_rows = lax.broadcasted_iota(jnp.int32, (16, 128), 0)
    mask_lanes = lax.broadcasted_iota(jnp.int32, (16, 128), 1)
    quad_mask = lax.rem(mask_rows, 4) == mask_lanes // 32
    low_half = lax.broadcasted_iota(jnp.int32, (8, 128), 0) < 4

    def iteration(i, carry):
        mean = state[0][0:1, 0:1] * (1.0 / CELLS) + 1e-6
        scale = jnp.sqrt(mean)
        inverse = 1.0 / scale

        def forward(cq, carry):
            def lift_pass(b, carry):
                x, y = lax.div(b, 16), pl.multiple_of(lax.rem(b, 16) * 8, 8)
                scaled = res[x, pl.ds(y, 8), :] * inverse
                logs = logp[x, pl.ds(y, 8), :]
                for c4 in range(4):
                    c = cq * 4 + c4
                    half = (lw[c, 0] * 0.5) * scaled + (lw[c, 1] * 0.5) * logs + lw[c, 2] * 0.5
                    inner = half * (2.0 * GELU_A + (8.0 * 0.044715 * GELU_A) * (half * half))
                    value = half + half * jnp.tanh(inner)
                    rest = value - value.astype(BF16).astype(F32)
                    lift[b, c] = jnp.concatenate([value, rest], axis=0).astype(BF16)
                return carry

            lax.fori_loop(0, 64, lift_pass, 0)
            tops, bottoms = [], []
            for c4 in range(4):
                c = cq * 4 + c4
                block = jnp.concatenate(
                    [lift[x * 16 : x * 16 + 16, c].reshape(256, NZ) for x in range(LX)], axis=1
                )
                deep = dot(block, tz[...]).reshape(16, 2, 8, 256)
                deep = (deep[:, 0] + deep[:, 1]).reshape(128, 256)
                tops.append(deep[:, :128])
                bottoms.append(deep[:, 128:])
            high, low = split(
                jnp.concatenate([jnp.concatenate(tops, axis=1), jnp.concatenate(bottoms, axis=1)], axis=0)
            )
            both = dot(yt[...], high)
            flat = both[:64] + both[64:] + dot(yt[0:64, :], low)
            for ri in range(2):
                square = jnp.concatenate(
                    [flat[ri * 32 : ri * 32 + 32, c4 * 128 : c4 * 128 + 128] for c4 in range(4)], axis=0
                )
                sf[cq, :, pl.ds(ri * 8, 8), :] = square.T.reshape(NR, 8, 128)
            vf[cq, row] = sf[cq, row]

            def step(k, carry):
                to = lax.rem(row + k, NR)
                send(sf.at[cq, to], vf.at[cq, row], f_s.at[cq], f_r.at[cq], to, col).start()
                return carry

            lax.fori_loop(1, NR, step, 0)
            return carry

        lax.fori_loop(0, 4, forward, 0)

        def point_pass(b, carry):
            x, y = lax.div(b, 16), lax.rem(b, 16)
            both = dot(maps[...], lift[b].reshape(256, NZ))
            point[x, y] = (both[:128] + both[128:]).reshape(CH, 8, NZ)
            return carry

        lax.fori_loop(0, 64, point_pass, 0)

        blocks = []
        for cq in range(4):
            whole = send(
                sf.at[cq, pl.ds(0, NR - 1)], vf.at[cq, pl.ds(0, NR - 1)], f_s.at[cq], f_r.at[cq], row, col
            )
            whole.wait_recv()
            whole.wait_send()
            blocks.append(vf[cq].reshape(256, 128))
        high, low = split(jnp.concatenate(blocks, axis=1))
        both = dot(xt[...], high)
        partial = both[:64] + both[64:] + dot(xt[0:64, :], low)
        sx[...] = partial.reshape(NC, 8, 512)
        vx[col] = sx[col]

        def scatter(k, carry):
            to = lax.rem(col + k, NC)
            send(sx.at[to], vx.at[col], x_s, x_r, row, to).start()
            return carry

        lax.fori_loop(1, NC, scatter, 0)
        whole = send(sx.at[pl.ds(0, NC - 1)], vx.at[pl.ds(0, NC - 1)], x_s, x_r, row, col)
        whole.wait_recv()
        whole.wait_send()
        spectrum = jnp.sum(vx[...], axis=0)

        stacks = []
        for ri in range(2):
            tiles = []
            for r in range(4):
                line = r * 2 + ri
                wide = [
                    jnp.broadcast_to(spectrum[line : line + 1, q * 128 : q * 128 + 128], (8, 128)) for q in range(4)
                ]
                tall = jnp.concatenate(
                    [jnp.where(low_half, wide[0], wide[1]), jnp.where(low_half, wide[2], wide[3])], axis=0
                )
                tiles.append(jnp.where(quad_mask, tall, 0.0))
            stacks.append(jnp.concatenate(tiles, axis=1))
        high, low = split(jnp.concatenate(stacks, axis=0))
        both = dot(jnp.concatenate([high, low], axis=0), fold[...])
        ordered = both[:32] + both[32:]

        reals, imags = [], []
        for kz in range(2):
            real = jnp.zeros((CH, 64), F32)
            imag = jnp.zeros((CH, 64), F32)
            for c in range(CH):
                value_real = ordered[c : c + 1, kz * 64 : kz * 64 + 64]
                value_imag = ordered[CH + c : CH + c + 1, kz * 64 : kz * 64 + 64]
                weight_real = weight[0, kz, c]
                weight_imag = weight[1, kz, c]
                real = real + (weight_real * value_real - weight_imag * value_imag)
                imag = imag + (weight_real * value_imag + weight_imag * value_real)
            reals.append(real)
            imags.append(imag)
        mixed = jnp.concatenate([jnp.concatenate(reals, axis=1), jnp.concatenate(imags, axis=1)], axis=0)

        high, low = split(mixed)
        both = dot(jnp.concatenate([high, low], axis=0), spread[...])
        wide = both[:32] + both[32:]
        mask = jnp.concatenate([quad_mask, quad_mask], axis=0)
        tall = jnp.concatenate(
            [jnp.where(mask, wide[:, r * 128 : r * 128 + 128], 0.0) for r in range(4)], axis=0
        )
        high, low = split(tall)
        both = dot(gather[...], jnp.concatenate([high, low], axis=1))
        sm[...] = (both[:, :128] + both[:, 128:]).reshape(4, 8, 128)
        vm[col] = sm[...]

        def spread_out(k, carry):
            send(sm, vm.at[col], m_s, m_r, row, lax.rem(col + k, NC)).start()
            return carry

        lax.fori_loop(1, NC, spread_out, 0)
        whole = send(vm.at[pl.ds(0, NC - 1)], vm.at[pl.ds(0, NC - 1)], m_s, m_r, row, col)
        whole.wait_recv()
        whole.wait_send()

        high, low = split(jnp.concatenate([vm[:, oq].reshape(64, 128) for oq in range(4)], axis=1))
        back = dot(xi[...], jnp.concatenate([high, low, high], axis=0))
        for oq in range(4):
            sh[oq] = back[:, oq * 128 : oq * 128 + 128].reshape(NR, 16, 128)
            vh[oq, row] = sh[oq, row]

            def step(k, carry, oq=oq):
                to = lax.rem(row + k, NR)
                send(sh.at[oq, to], vh.at[oq, row], h_s.at[oq], h_r.at[oq], to, col).start()
                return carry

            lax.fori_loop(1, NR, step, 0)

        def clear(b, carry):
            x, y = lax.div(b, 4), pl.multiple_of(lax.rem(b, 4) * 32, 32)
            padk[x + 1, pl.ds(pl.multiple_of(y + 8, 8), 32), :] = jnp.full((32, NZ), pw[CH], F32)
            return carry

        lax.fori_loop(0, 16, clear, 0)

        def backward(oq, carry):
            whole = send(
                sh.at[oq, pl.ds(0, NR - 1)], vh.at[oq, pl.ds(0, NR - 1)], h_s.at[oq], h_r.at[oq], row, col
            )
            whole.wait_recv()
            whole.wait_send()
            turned = [vh[oq, :, pl.ds(ri * 8, 8), :].reshape(128, 128).T for ri in range(2)]
            block = jnp.concatenate(
                [
                    jnp.concatenate([turned[ri][o4 * 32 : o4 * 32 + 32] for ri in range(2)], axis=0)
                    for o4 in range(4)
                ],
                axis=1,
            )
            high, low = split(block)
            back = dot(yi[...], jnp.concatenate([high, low, high], axis=0))
            for o4 in range(4):
                part = back[:, o4 * 128 : o4 * 128 + 128]
                high, low = split(jnp.concatenate([part[:128], part[128:]], axis=1))
                modes[o4] = jnp.concatenate([high, low, high], axis=1)

            for x in range(LX):
                for o4 in range(4):
                    o = oq * 4 + o4
                    bias = mw[o, CH] * 0.5
                    weight_out = pw[o]
                    wave = dot(modes[o4], ti[:, x * NZ : x * NZ + NZ])
                    half = wave + point[x, :, o].reshape(128, NZ) + bias
                    inner = half * (2.0 * GELU_A + (8.0 * 0.044715 * GELU_A) * (half * half))
                    hidden = weight_out * (half + half * jnp.tanh(inner))
                    padk[x + 1, pl.ds(8, LY), :] += hidden
            return carry

        lax.fori_loop(0, 4, backward, 0)

        def finish(b, carry):
            x, y = lax.div(b, 4), pl.multiple_of(lax.rem(b, 4) * 32, 32)
            value = scale * padk[x + 1, pl.ds(pl.multiple_of(y + 8, 8), 32), :]
            padk[x + 1, pl.ds(pl.multiple_of(y + 8, 8), 32), :] = value
            kept[i, x, pl.ds(y, 32), :] = value
            return carry

        lax.fori_loop(0, 16, finish, 0)

        copies = [
            send(padk.at[LX, pl.ds(8, LY)], padk.at[0, pl.ds(8, LY)], halo_s.at[0], halo_r.at[0], up_row, col),
            send(padk.at[1, pl.ds(8, LY)], padk.at[LX + 1, pl.ds(8, LY)], halo_s.at[1], halo_r.at[1], down_row, col),
            send(
                padk.at[pl.ds(1, LX), pl.ds(LY, 8)], padk.at[pl.ds(1, LX), pl.ds(0, 8)],
                halo_s.at[2], halo_r.at[2], row, up_col,
            ),
            send(
                padk.at[pl.ds(1, LX), pl.ds(8, 8)], padk.at[pl.ds(1, LX), pl.ds(LY + 8, 8)],
                halo_s.at[3], halo_r.at[3], row, down_col,
            ),
        ]
        for copy in copies:
            copy.start()
        for copy in copies:
            copy.wait()

        @pl.when(row == 0)
        def _():
            padk[0, pl.ds(8, LY), :] = jnp.zeros((LY, NZ), F32)

        @pl.when(row == NR - 1)
        def _():
            padk[LX + 1, pl.ds(8, LY), :] = jnp.zeros((LY, NZ), F32)

        @pl.when(col == 0)
        def _():
            padk[pl.ds(1, LX), pl.ds(0, 8), :] = jnp.zeros((LX, 8, NZ), F32)

        @pl.when(col == NC - 1)
        def _():
            padk[pl.ds(1, LX), pl.ds(LY + 8, 8), :] = jnp.zeros((LX, 8, NZ), F32)

        def fold8(value):
            return (value[0:8] + value[8:16]) + (value[16:24] + value[24:32])

        def operator_pass(b, totals):
            x, y = lax.div(b, 4), pl.multiple_of(lax.rem(b, 4) * 32, 32)
            here, others = around(padk, x, y, False)
            applied = jnp.zeros((32, NZ), F32)
            for n, other in enumerate(others):
                applied = applied + faces[n, x, pl.ds(y, 32), :] * (here - other)
            fresh[x, pl.ds(y, 32), :] = applied
            old_image = image[x, pl.ds(y, 32), :]
            residual = res[x, pl.ds(y, 32), :]
            old = prev[x, pl.ds(y, 32), :]
            terms = (
                here * applied, here * old_image, residual * here, residual * old, residual * applied,
                applied * applied,
            )
            return tuple(total + fold8(term) for total, term in zip(totals, terms))

        totals = lax.fori_loop(0, 16, operator_pass, tuple(jnp.zeros((8, NZ), F32) for _ in range(6)))
        sums_begin(1 + i, tile_of(totals))
        sums = sums_end(1 + i)
        k_ak, k_img, r_k, r_d, r_ak, ak_ak = [sums[n : n + 1] for n in range(6)]
        old_curve = state[1][0:1, 0:1]
        beta = k_img / old_curve
        curve = k_ak - 2.0 * beta * k_img + beta * beta * old_curve
        alpha = (r_k - beta * r_d) / curve

        def update(b, carry):
            x, y = lax.div(b, 4), pl.multiple_of(lax.rem(b, 4) * 32, 32)
            at = (x, pl.ds(y, 32), slice(None))
            direction = padk[x + 1, pl.ds(pl.multiple_of(y + 8, 8), 32), :] - beta * prev[at]
            applied = fresh[at] - beta * image[at]
            prev[at] = direction
            image[at] = applied
            sol[at] = sol[at] + alpha * direction
            res[at] = res[at] - alpha * applied
            return carry

        lax.fori_loop(0, 16, update, 0)
        squares = state[0][0:1, 0:1] - 2.0 * alpha * r_ak + alpha * alpha * ak_ak
        state[0] = jnp.broadcast_to(jnp.maximum(squares, 0.0), (8, 128))
        state[1] = jnp.broadcast_to(curve, (8, 128))
        return carry

    lax.fori_loop(0, 2, iteration, 0)


def local(right_side, permeability, lift_weight, spectral_weight, mix_weight, proj_weight):
    vmem = pl.BlockSpec(memory_space=pltpu.VMEM)
    smem = pl.BlockSpec(memory_space=pltpu.SMEM)
    hbm = pl.BlockSpec(memory_space=pl.ANY)
    field = (LX, LY, NZ)
    dma = pltpu.SemaphoreType.DMA
    scratch = [
        pltpu.VMEM((64, CH, 16, NZ), BF16),
        pltpu.VMEM((LX, 16, CH, 8, NZ), F32),
        pltpu.VMEM(field, F32),
        pltpu.VMEM((LX + 2, LY + 16, NZ), F32),
        pltpu.VMEM((LX + 2, LY + 16, NZ), F32),
        pltpu.VMEM((6,) + field, F32),
        pltpu.VMEM(field, F32),
        pltpu.VMEM(field, F32),
        pltpu.VMEM(field, F32),
        pltpu.VMEM((256, 256), BF16),
        pltpu.VMEM((128, 256), BF16),
        pltpu.VMEM((256, 192), BF16),
        pltpu.VMEM((LY, NZ), BF16),
        pltpu.VMEM((LY, NZ), BF16),
        pltpu.VMEM((LX, 16, NZ), BF16),
        pltpu.VMEM((LX, 16, NZ), BF16),
        pltpu.VMEM((4, NR, 16, 128), F32),
        pltpu.VMEM((4, NR, 16, 128), F32),
        pltpu.VMEM((NC, 8, 512), F32),
        pltpu.VMEM((NC, 8, 512), F32),
        pltpu.VMEM((4, 8, 128), F32),
        pltpu.VMEM((NC, 4, 8, 128), F32),
        pltpu.VMEM((4, NR, 16, 128), F32),
        pltpu.VMEM((4, NR, 16, 128), F32),
        pltpu.VMEM((4, LY, 768), BF16),
        pltpu.VMEM((3, 8, 128), F32),
        pltpu.VMEM((3, NC, 8, 128), F32),
        pltpu.VMEM((3, 8, 128), F32),
        pltpu.VMEM((3, NR, 8, 128), F32),
        pltpu.VMEM((2, 8, 128), F32),
        dma((4,)), dma((4,)), dma((4,)), dma((4,)), dma((4,)), dma((4,)),
        dma, dma, dma, dma, dma((4,)), dma((4,)),
        dma((3,)), dma((3,)), dma((3,)), dma((3,)), dma((2,)),
    ]
    constants = [jnp.asarray(t) for t in tables()]
    return pl.pallas_call(
        kernel,
        out_shape=[
            jax.ShapeDtypeStruct(field, F32),
            jax.ShapeDtypeStruct(field, F32),
            jax.ShapeDtypeStruct((2,) + field, F32),
        ],
        in_specs=[vmem, vmem, smem, smem, smem, vmem, vmem, vmem, vmem, hbm, hbm] + [vmem] * 7,
        out_specs=[vmem, vmem, vmem],
        scratch_shapes=scratch,
        compiler_params=pltpu.CompilerParams(
            collective_id=0, has_side_effects=True, vmem_limit_bytes=56 * 1024 * 1024
        ),
    )(
        right_side, permeability, lift_weight, mix_weight, proj_weight, mix_weight,
        spectral_weight, *constants,
    )


def solution(mesh):
    placed = (
        P("row", "col", None), P("row", "col", None), P(), P(None, "row", None, None, "col"), P(), P(),
    )
    return jax.shard_map(
        local,
        mesh=mesh,
        in_specs=placed,
        out_specs=(P("row", "col", None), P("row", "col", None), P(None, "row", "col", None)),
        check_vma=False,
    )
```

```python
import jax
import jax.numpy as jnp
import ml_dtypes
import numpy as np
from jax import lax
from jax.experimental import pallas as pl
from jax.experimental.pallas import tpu as pltpu
from jax.sharding import PartitionSpec as P

F32 = jnp.float32
BF16 = jnp.bfloat16
MESH = pl.DeviceIdType.MESH
NR, NC = 16, 8
NX, NY, NZ = 64, 1024, 256
LX, LY = NX // NR, NY // NC
CH = 16
CELLS = float(NX * NY * NZ)
GELU_A = float(np.sqrt(2.0 / np.pi))


def pieces(table):
    high = table.astype(ml_dtypes.bfloat16)
    low = (table - high.astype(np.float64)).astype(ml_dtypes.bfloat16)
    return high, low


def waves(freqs, places, length):
    angle = 2.0 * np.pi * ((freqs[None, :] * places[:, None]) % length) / length
    return np.cos(angle), np.sin(angle)


def tables():
    cz, sz = waves(np.arange(32), np.arange(NZ), NZ)
    tz = np.zeros((LX, NZ, 2, 32, LX))
    ti = np.zeros((2, 32, LX, LX, NZ))
    for x in range(LX):
        tz[x, :, 0, :, x] = cz
        tz[x, :, 1, :, x] = sz
        ti[0, :, x, x, :] = cz.T
        ti[1, :, x, x, :] = -sz.T
    tz = pieces(tz.reshape(LX * NZ, 256))[0]
    ti_high, ti_low = pieces(ti.reshape(256, LX * NZ))
    ti = np.concatenate([ti_high, ti_high, ti_low], axis=0)
    ti = np.ascontiguousarray(ti.reshape(768, LX, NZ).transpose(1, 0, 2))

    yt = np.zeros((NC, 2, 32, 2, LY))
    yi = np.zeros((NC, 2, LY, 2, 32))
    for col in range(NC):
        cy, sy = waves(np.arange(-16, 16), np.arange(LY) + col * LY, NY)
        yt[col, 0, :, 0] = cy.T
        yt[col, 0, :, 1] = -sy.T
        yt[col, 1, :, 0] = -sy.T
        yt[col, 1, :, 1] = -cy.T
        yi[col, 0, :, 0] = cy
        yi[col, 0, :, 1] = -sy
        yi[col, 1, :, 0] = sy
        yi[col, 1, :, 1] = cy
    yt = np.concatenate(pieces(yt.reshape(NC, 64, 256)), axis=1)
    yi_high, yi_low = pieces(yi.reshape(NC, 256, 64))
    yi = np.concatenate([yi_high, yi_high, yi_low], axis=2)

    cx, sx = waves(np.arange(-8, 8), np.arange(NX), NX)
    cx = cx.reshape(NR, LX, NC, 2)
    sx = sx.reshape(NR, LX, NC, 2)
    xt = np.zeros((NC, 2, 2, 2, NR, 2, 2, LX))
    xi = np.zeros((NR, 2, 2, LX, NC, 2, 2, 2))
    for kz in range(2):
        forward_cos = cx.transpose(2, 3, 0, 1)
        forward_sin = sx.transpose(2, 3, 0, 1)
        xt[:, kz, :, 0, :, 0, kz, :] = forward_cos
        xt[:, kz, :, 0, :, 1, kz, :] = forward_sin
        xt[:, kz, :, 1, :, 1, kz, :] = forward_cos
        xt[:, kz, :, 1, :, 0, kz, :] = -forward_sin
        xi[:, 0, kz, :, :, kz, :, 0] = cx
        xi[:, 0, kz, :, :, kz, :, 1] = -sx
        xi[:, 1, kz, :, :, kz, :, 1] = cx
        xi[:, 1, kz, :, :, kz, :, 0] = sx
    xt = np.concatenate(pieces(xt.reshape(64, 256)), axis=0)
    xi_high, xi_low = pieces(xi.reshape(256, 64) * (0.5 / CELLS))
    xi = np.concatenate([xi_high, xi_high, xi_low], axis=1)

    fold = np.zeros((4, 4, 32, 4, 32))
    for r in range(4):
        for c in range(4):
            fold[r, c, :, r, :] = np.eye(32)
    fold = fold.reshape(512, 128)
    spread = np.ascontiguousarray(fold.T)
    gather = np.zeros((4, 4, 2, 4, 2, 16))
    for quad in range(4):
        for r in range(4):
            for ri in range(2):
                gather[quad, r, ri, r, ri, quad * 4 : quad * 4 + 4] = 1.0
    gather = gather.reshape(32, 128)
    left = np.kron(np.eye(16), np.ones((8, 1)))
    right = np.zeros((16, 16, 2, 8))
    for c in range(16):
        right[c, c] = 1.0
    right = right.reshape(16, 256)
    b16 = lambda a: a.astype(ml_dtypes.bfloat16)
    return tz, ti, yt, yi, xt, xi, b16(fold), b16(spread), b16(gather), b16(left), b16(right)


def split(value):
    high = value.astype(BF16)
    return high, (value - high.astype(F32)).astype(BF16)


def dot(left, right):
    return jnp.dot(left, right, preferred_element_type=F32)


def kernel(
    rs, perm_in, lw, mw, pw, mix_in, weight_in,
    tz_in, ti_in, yt_all, yi_all, xt_in, xi_in, fold_in, spread_in, gather_in, left_in, right_in,
    kept_out, image_out, steps_out,
    res, perm, mixv, weight, tz, ti, xt, xi, fold, spread, gather, left_map, right_map,
    lift, point, logp, padk, padp, faces, prev, image, fresh, maps, yt, yi,
    plx, phx, ply, phy,
    sf, vf, sx, vx, sm, vm, sh, vh, modes,
    asrc, acol, bsrc, arow, state,
    perm_s, perm_r, halo_s, halo_r, f_s, f_r, x_s, x_r, m_s, m_r, h_s, h_r, ac_s, ac_r, ar_s, ar_r, table_s, kept_s, image_s,
):
    row = lax.axis_index("row")
    col = lax.axis_index("col")
    up_row, down_row = lax.rem(row + 1, NR), lax.rem(row + NR - 1, NR)
    up_col, down_col = lax.rem(col + 1, NC), lax.rem(col + NC - 1, NC)

    def send(src, dst, s, r, to_row, to_col):
        return pltpu.make_async_remote_copy(
            src_ref=src, dst_ref=dst, send_sem=s, recv_sem=r, device_id=(to_row, to_col), device_id_type=MESH
        )

    loads = [
        (rs, res), (perm_in, perm), (mix_in, mixv), (left_in, left_map), (right_in, right_map), (tz_in, tz),
        (yt_all.at[col], yt), (xt_in, xt), (weight_in, weight), (fold_in, fold), (spread_in, spread),
        (gather_in, gather), (xi_in, xi), (yi_all.at[col], yi), (ti_in, ti),
    ]
    loads = [pltpu.make_async_copy(src, dst, table_s.at[n]) for n, (src, dst) in enumerate(loads)]
    for copy in loads:
        copy.start()

    barrier = pltpu.get_barrier_semaphore()

    def greet_row(k, carry):
        pl.semaphore_signal(barrier, 1, device_id=(lax.rem(row + k, NR), col), device_id_type=MESH)
        return carry

    def greet_col(k, carry):
        pl.semaphore_signal(barrier, 1, device_id=(row, lax.rem(col + k, NC)), device_id_type=MESH)
        return carry

    lax.fori_loop(1, NR, greet_row, 0, unroll=True)
    lax.fori_loop(1, NC, greet_col, 0, unroll=True)
    pl.semaphore_wait(barrier, NR + NC - 2)

    perm_copies = [
        send(perm_in.at[LX - 1], plx, perm_s.at[0], perm_r.at[0], up_row, col),
        send(perm_in.at[0], phx, perm_s.at[1], perm_r.at[1], down_row, col),
        send(perm_in.at[:, pl.ds(LY - 16, 16), :], ply, perm_s.at[2], perm_r.at[2], row, up_col),
        send(perm_in.at[:, pl.ds(0, 16), :], phy, perm_s.at[3], perm_r.at[3], row, down_col),
    ]
    for copy in perm_copies:
        copy.start()

    def sums_begin(u, tile):
        asrc[u] = tile
        acol[u, col] = tile

        def step(k, carry):
            send(asrc.at[u], acol.at[u, col], ac_s.at[u], ac_r.at[u], row, lax.rem(col + k, NC)).start()
            return carry

        lax.fori_loop(1, NC, step, 0, unroll=True)

    def sums_end(u):
        whole = send(acol.at[u, pl.ds(0, NC - 1)], acol.at[u, pl.ds(0, NC - 1)], ac_s.at[u], ac_r.at[u], row, col)
        whole.wait_recv()
        whole.wait_send()
        tile = jnp.sum(acol[u], axis=0)
        bsrc[u] = tile
        arow[u, row] = tile

        def step(k, carry):
            send(bsrc.at[u], arow.at[u, row], ar_s.at[u], ar_r.at[u], lax.rem(row + k, NR), col).start()
            return carry

        lax.fori_loop(1, NR, step, 0, unroll=True)
        whole = send(arow.at[u, pl.ds(0, NR - 1)], arow.at[u, pl.ds(0, NR - 1)], ar_s.at[u], ar_r.at[u], row, col)
        whole.wait_recv()
        whole.wait_send()
        return jnp.sum(jnp.sum(arow[u], axis=0), axis=1, keepdims=True)

    def tile_of(parts):
        rows = []
        for part in parts:
            line = jnp.sum(part, axis=0, keepdims=True)
            rows.append(line[:, :128] + line[:, 128:])
        index = lax.broadcasted_iota(jnp.int32, (8, 128), 0)
        tile = jnp.zeros((8, 128), F32)
        for i, line in enumerate(rows):
            tile = jnp.where(index == i, jnp.broadcast_to(line, (8, 128)), tile)
        return tile

    def first_pass(b, total):
        x, y = lax.div(b, 4), pl.multiple_of(lax.rem(b, 4) * 32, 32)
        value = res[x, pl.ds(y, 32), :]
        squares = value * value
        return total + (squares[0:8] + squares[8:16]) + (squares[16:24] + squares[24:32])

    loads[0].wait()
    total = lax.fori_loop(0, 16, first_pass, jnp.zeros((8, NZ), F32))
    sums_begin(0, tile_of([total]))

    def second_pass(b, carry):
        x, y = lax.div(b, 4), pl.multiple_of(lax.rem(b, 4) * 32, 32)
        value = perm[x, pl.ds(y, 32), :].astype(F32)
        padp[x + 1, pl.ds(pl.multiple_of(y + 8, 8), 32), :] = value
        logp[x, pl.ds(y, 32), :] = jnp.log(value)
        zero = jnp.zeros((32, NZ), F32)
        prev[x, pl.ds(y, 32), :] = zero
        image[x, pl.ds(y, 32), :] = zero
        return carry

    for copy in loads[1:5]:
        copy.wait()
    lax.fori_loop(0, 16, second_pass, 0)
    mix_high, mix_low = split(mixv[:, 0:CH] * 0.5)
    rows_iota = lax.broadcasted_iota(jnp.int32, (128, 256), 0)
    lane_iota = lax.broadcasted_iota(jnp.int32, (128, 256), 1)
    same = lax.rem(rows_iota, 8) == lax.rem(lane_iota, 8)
    for n, piece in enumerate((mix_high, mix_low)):
        wide = dot(left_map[...], dot(piece, right_map[...]).astype(BF16))
        maps[n * 128 : (n + 1) * 128, :] = jnp.where(same, wide, 0.0).astype(BF16)

    lanes = lax.broadcasted_iota(jnp.int32, (32, NZ), 1)

    def around(ref, x, y, edge):
        own = ref[x + 1, pl.ds(y, 48), :]
        here = own[8:40]
        before = pltpu.roll(here, 1, 1)
        after = pltpu.roll(here, NZ - 1, 1)
        if edge:
            before = jnp.where(lanes == 0, here, before)
            after = jnp.where(lanes == NZ - 1, here, after)
        else:
            before = jnp.where(lanes == 0, 0.0, before)
            after = jnp.where(lanes == NZ - 1, 0.0, after)
        return here, (
            ref[x, pl.ds(pl.multiple_of(y + 8, 8), 32), :], ref[x + 2, pl.ds(pl.multiple_of(y + 8, 8), 32), :], own[7:39], own[9:41], before, after
        )

    def build_faces():
        for copy in perm_copies:
            copy.wait()
        padp[0, pl.ds(8, LY), :] = plx[...].astype(F32)
        padp[LX + 1, pl.ds(8, LY), :] = phx[...].astype(F32)
        for x in range(LX):
            padp[x + 1, pl.ds(0, 8), :] = ply[x].astype(F32)[8:16]
            padp[x + 1, pl.ds(LY + 8, 8), :] = phy[x].astype(F32)[0:8]

        @pl.when(row == 0)
        def _():
            padp[0, pl.ds(8, LY), :] = padp[1, pl.ds(8, LY), :]

        @pl.when(row == NR - 1)
        def _():
            padp[LX + 1, pl.ds(8, LY), :] = padp[LX, pl.ds(8, LY), :]

        @pl.when(col == 0)
        def _():
            for x in range(LX):
                padp[x + 1, pl.ds(0, 8), :] = jnp.broadcast_to(padp[x + 1, pl.ds(8, 8), :][0:1], (8, NZ))

        @pl.when(col == NC - 1)
        def _():
            for x in range(LX):
                padp[x + 1, pl.ds(LY + 8, 8), :] = jnp.broadcast_to(padp[x + 1, pl.ds(LY, 8), :][7:8], (8, NZ))

        def face_pass(b, carry):
            x, y = lax.div(b, 4), pl.multiple_of(lax.rem(b, 4) * 32, 32)
            here, others = around(padp, x, y, True)
            for n, other in enumerate(others):
                faces[n, x, pl.ds(y, 32), :] = 2.0 * here * other / (here + other)
            return carry

        lax.fori_loop(0, 16, face_pass, 0)

    for copy in loads[5:]:
        copy.wait()
    state[0] = jnp.broadcast_to(sums_end(0)[0:1], (8, 128))
    state[1] = jnp.ones((8, 128), F32)

    mask_rows = lax.broadcasted_iota(jnp.int32, (16, 128), 0)
    mask_lanes = lax.broadcasted_iota(jnp.int32, (16, 128), 1)
    quad_mask = lax.rem(mask_rows, 4) == mask_lanes // 32
    low_half = lax.broadcasted_iota(jnp.int32, (8, 128), 0) < 4

    def iteration(i, carry):
        mean = state[0][0:1, 0:1] * (1.0 / CELLS) + 1e-6
        scale = jnp.sqrt(mean)
        inverse = 1.0 / scale

        def along_x(cq):
            whole = send(
                sf.at[cq, pl.ds(0, NR - 1)], vf.at[cq, pl.ds(0, NR - 1)], f_s.at[cq], f_r.at[cq], row, col
            )
            whole.wait_recv()
            whole.wait_send()
            high, low = split(vf[cq].reshape(256, 128))
            both = dot(xt[...], high)
            sx[cq] = (both[:64] + both[64:] + dot(xt[0:64, :], low)).reshape(NC, 8, 128)
            vx[cq, col] = sx[cq, col]

            def scatter(k, carry):
                to = lax.rem(col + k, NC)
                send(sx.at[cq, to], vx.at[cq, col], x_s.at[cq], x_r.at[cq], row, to).start()
                return carry

            lax.fori_loop(1, NC, scatter, 0, unroll=True)

        def forward(cq, carry):
            def lift_pass(b, carry):
                x, y = lax.div(b, 16), pl.multiple_of(lax.rem(b, 16) * 8, 8)
                scaled = res[x, pl.ds(y, 8), :] * inverse
                logs = logp[x, pl.ds(y, 8), :]
                for c4 in range(4):
                    c = cq * 4 + c4
                    half = (lw[0, c] * 0.5) * scaled + (lw[1, c] * 0.5) * logs + lw[2, c] * 0.5
                    inner = half * (2.0 * GELU_A + (8.0 * 0.044715 * GELU_A) * (half * half))
                    value = half + half * jnp.tanh(inner)
                    rest = value - value.astype(BF16).astype(F32)
                    lift[b, c] = jnp.concatenate([value, rest], axis=0).astype(BF16)
                return carry

            lax.fori_loop(0, 64, lift_pass, 0, unroll=8)
            tops, bottoms = [], []
            for c4 in range(4):
                c = cq * 4 + c4
                block = jnp.concatenate(
                    [lift[x * 16 : x * 16 + 16, c].reshape(256, NZ) for x in range(LX)], axis=1
                )
                deep = dot(block, tz[...]).reshape(16, 2, 8, 256)
                deep = (deep[:, 0] + deep[:, 1]).reshape(128, 256)
                tops.append(deep[:, :128])
                bottoms.append(deep[:, 128:])
            high, low = split(
                jnp.concatenate([jnp.concatenate(tops, axis=1), jnp.concatenate(bottoms, axis=1)], axis=0)
            )
            both = dot(yt[...], high)
            flat = both[:64] + both[64:] + dot(yt[0:64, :], low)
            turned = []
            for ri in range(2):
                square = jnp.concatenate(
                    [flat[ri * 32 : ri * 32 + 32, c4 * 128 : c4 * 128 + 128] for c4 in range(4)], axis=0
                )
                turned.append(square.T.reshape(NR, 8, 128))
            sf[cq] = jnp.concatenate(turned, axis=1)
            vf[cq, row] = sf[cq, row]

            def step(k, carry):
                to = lax.rem(row + k, NR)
                send(sf.at[cq, to], vf.at[cq, row], f_s.at[cq], f_r.at[cq], to, col).start()
                return carry

            lax.fori_loop(1, NR, step, 0, unroll=True)

            return carry

        lax.fori_loop(0, 4, forward, 0)
        for cq in range(4):
            along_x(cq)

        @pl.when(i == 0)
        def _():
            build_faces()


        spectrum = []
        for cq in range(4):
            whole = send(
                sx.at[cq, pl.ds(0, NC - 1)], vx.at[cq, pl.ds(0, NC - 1)], x_s.at[cq], x_r.at[cq], row, col
            )
            whole.wait_recv()
            whole.wait_send()
            spectrum.append(jnp.sum(vx[cq], axis=0))

        stacks = []
        for ri in range(2):
            tiles = []
            for r in range(4):
                line = r * 2 + ri
                wide = [
                    jnp.broadcast_to(spectrum[q][line : line + 1], (8, 128)) for q in range(4)
                ]
                tall = jnp.concatenate(
                    [jnp.where(low_half, wide[0], wide[1]), jnp.where(low_half, wide[2], wide[3])], axis=0
                )
                tiles.append(jnp.where(quad_mask, tall, 0.0))
            stacks.append(jnp.concatenate(tiles, axis=1))
        high, low = split(jnp.concatenate(stacks, axis=0))
        both = dot(jnp.concatenate([high, low], axis=0), fold[...])
        ordered = both[:32] + both[32:]

        reals, imags = [], []
        for kz in range(2):
            real = jnp.zeros((CH, 64), F32)
            imag = jnp.zeros((CH, 64), F32)
            for c in range(CH):
                value_real = ordered[c : c + 1, kz * 64 : kz * 64 + 64]
                value_imag = ordered[CH + c : CH + c + 1, kz * 64 : kz * 64 + 64]
                weight_real = weight[0, kz, c]
                weight_imag = weight[1, kz, c]
                real = real + (weight_real * value_real - weight_imag * value_imag)
                imag = imag + (weight_real * value_imag + weight_imag * value_real)
            reals.append(real)
            imags.append(imag)
        mixed = jnp.concatenate([jnp.concatenate(reals, axis=1), jnp.concatenate(imags, axis=1)], axis=0)

        high, low = split(mixed)
        both = dot(jnp.concatenate([high, low], axis=0), spread[...])
        wide = both[:32] + both[32:]
        mask = jnp.concatenate([quad_mask, quad_mask], axis=0)
        tall = jnp.concatenate(
            [jnp.where(mask, wide[:, r * 128 : r * 128 + 128], 0.0) for r in range(4)], axis=0
        )
        high, low = split(tall)
        both = dot(gather[...], jnp.concatenate([high, low], axis=1))
        sm[...] = (both[:, :128] + both[:, 128:]).reshape(4, 8, 128)
        vm[col] = sm[...]

        def spread_out(k, carry):
            send(sm, vm.at[col], m_s, m_r, row, lax.rem(col + k, NC)).start()
            return carry

        lax.fori_loop(1, NC, spread_out, 0, unroll=True)
        whole = send(vm.at[pl.ds(0, NC - 1)], vm.at[pl.ds(0, NC - 1)], m_s, m_r, row, col)
        whole.wait_recv()
        whole.wait_send()

        high, low = split(jnp.concatenate([vm[:, oq].reshape(64, 128) for oq in range(4)], axis=1))
        back = dot(xi[...], jnp.concatenate([high, low, high], axis=0))
        for oq in range(4):
            sh[oq] = back[:, oq * 128 : oq * 128 + 128].reshape(NR, 16, 128)
            vh[oq, row] = sh[oq, row]

            def step(k, carry, oq=oq):
                to = lax.rem(row + k, NR)
                send(sh.at[oq, to], vh.at[oq, row], h_s.at[oq], h_r.at[oq], to, col).start()
                return carry

            lax.fori_loop(1, NR, step, 0, unroll=True)

        def point_pass(b, carry):
            x, y = lax.div(b, 16), lax.rem(b, 16)
            both = dot(maps[...], lift[b].reshape(256, NZ))
            point[x, y] = (both[:128] + both[128:]).reshape(CH, 8, NZ)
            return carry

        lax.fori_loop(0, 64, point_pass, 0, unroll=8)

        def clear(b, carry):
            x, y = lax.div(b, 4), pl.multiple_of(lax.rem(b, 4) * 32, 32)
            padk[x + 1, pl.ds(pl.multiple_of(y + 8, 8), 32), :] = jnp.full((32, NZ), pw[CH], F32)
            return carry

        lax.fori_loop(0, 16, clear, 0)

        def backward(oq, carry):
            whole = send(
                sh.at[oq, pl.ds(0, NR - 1)], vh.at[oq, pl.ds(0, NR - 1)], h_s.at[oq], h_r.at[oq], row, col
            )
            whole.wait_recv()
            whole.wait_send()
            turned = [vh[oq, :, pl.ds(ri * 8, 8), :].reshape(128, 128).T for ri in range(2)]
            block = jnp.concatenate(
                [
                    jnp.concatenate([turned[ri][o4 * 32 : o4 * 32 + 32] for ri in range(2)], axis=0)
                    for o4 in range(4)
                ],
                axis=1,
            )
            high, low = split(block)
            back = dot(yi[...], jnp.concatenate([high, low, high], axis=0))
            for o4 in range(4):
                part = back[:, o4 * 128 : o4 * 128 + 128]
                high, low = split(jnp.concatenate([part[:128], part[128:]], axis=1))
                modes[oq * 4 + o4] = jnp.concatenate([high, low, high], axis=1)
            return carry

        lax.fori_loop(0, 4, backward, 0)

        def planes(xs):
            def channels(oq, carry):
                for x in xs:
                    for o4 in range(4):
                        o = oq * 4 + o4
                        bias = mw[o, CH] * 0.5
                        wave = dot(modes[o], ti[x])
                        half = wave + point[x, :, o].reshape(LY, NZ) + bias
                        inner = half * (2.0 * GELU_A + (8.0 * 0.044715 * GELU_A) * (half * half))
                        hidden = pw[o] * (half + half * jnp.tanh(inner))
                        padk[x + 1, pl.ds(8, LY), :] += hidden
                return carry

            lax.fori_loop(0, 4, channels, 0)
            for x in xs:
                padk[x + 1, pl.ds(8, LY), :] = scale * padk[x + 1, pl.ds(8, LY), :]

        planes((0, LX - 1))
        copies = [
            send(padk.at[LX, pl.ds(8, LY)], padk.at[0, pl.ds(8, LY)], halo_s.at[0], halo_r.at[0], up_row, col),
            send(padk.at[1, pl.ds(8, LY)], padk.at[LX + 1, pl.ds(8, LY)], halo_s.at[1], halo_r.at[1], down_row, col),
            send(
                padk.at[pl.ds(1, LX), pl.ds(LY, 8)], padk.at[pl.ds(1, LX), pl.ds(0, 8)],
                halo_s.at[2], halo_r.at[2], row, up_col,
            ),
            send(
                padk.at[pl.ds(1, LX), pl.ds(8, 8)], padk.at[pl.ds(1, LX), pl.ds(LY + 8, 8)],
                halo_s.at[3], halo_r.at[3], row, down_col,
            ),
        ]
        for copy in copies[:2]:
            copy.start()
        planes(range(1, LX - 1))
        for copy in copies[2:]:
            copy.start()
        keep = pltpu.make_async_copy(padk.at[pl.ds(1, LX), pl.ds(8, LY)], kept_out.at[i], kept_s)
        keep.start()
        for copy in copies:
            copy.wait()

        @pl.when(row == 0)
        def _():
            padk[0, pl.ds(8, LY), :] = jnp.zeros((LY, NZ), F32)

        @pl.when(row == NR - 1)
        def _():
            padk[LX + 1, pl.ds(8, LY), :] = jnp.zeros((LY, NZ), F32)

        @pl.when(col == 0)
        def _():
            padk[pl.ds(1, LX), pl.ds(0, 8), :] = jnp.zeros((LX, 8, NZ), F32)

        @pl.when(col == NC - 1)
        def _():
            padk[pl.ds(1, LX), pl.ds(LY + 8, 8), :] = jnp.zeros((LX, 8, NZ), F32)

        def fold8(value):
            return (value[0:8] + value[8:16]) + (value[16:24] + value[24:32])

        def operator_pass(b, totals):
            x, y = lax.div(b, 4), pl.multiple_of(lax.rem(b, 4) * 32, 32)
            here, others = around(padk, x, y, False)
            applied = jnp.zeros((32, NZ), F32)
            for n, other in enumerate(others):
                applied = applied + faces[n, x, pl.ds(y, 32), :] * (here - other)
            fresh[x, pl.ds(y, 32), :] = applied
            old_image = image[x, pl.ds(y, 32), :]
            residual = res[x, pl.ds(y, 32), :]
            old = prev[x, pl.ds(y, 32), :]
            terms = (
                here * applied, here * old_image, residual * here, residual * old, residual * applied,
                applied * applied,
            )
            return tuple(total + fold8(term) for total, term in zip(totals, terms))

        totals = lax.fori_loop(0, 16, operator_pass, tuple(jnp.zeros((8, NZ), F32) for _ in range(6)))
        sums_begin(1 + i, tile_of(totals))
        sums = sums_end(1 + i)
        k_ak, k_img, r_k, r_d, r_ak, ak_ak = [sums[n : n + 1] for n in range(6)]
        old_curve = state[1][0:1, 0:1]
        beta = k_img / old_curve
        curve = k_ak - 2.0 * beta * k_img + beta * beta * old_curve
        alpha = (r_k - beta * r_d) / curve

        show = pltpu.make_async_copy(fresh, image_out.at[i], image_s)
        show.start()

        @pl.when(i == 0)
        def _():
            def update(b, carry):
                x, y = lax.div(b, 4), pl.multiple_of(lax.rem(b, 4) * 32, 32)
                at = (x, pl.ds(y, 32), slice(None))
                applied = fresh[at]
                prev[at] = padk[x + 1, pl.ds(pl.multiple_of(y + 8, 8), 32), :]
                image[at] = applied
                res[at] = res[at] - alpha * applied
                return carry

            lax.fori_loop(0, 16, update, 0)

        steps_out[i] = jnp.broadcast_to(alpha, (8, 128))
        steps_out[2 + i] = jnp.broadcast_to(beta, (8, 128))
        keep.wait()
        show.wait()
        squares = state[0][0:1, 0:1] - 2.0 * alpha * r_ak + alpha * alpha * ak_ak
        state[0] = jnp.broadcast_to(jnp.maximum(squares, 0.0), (8, 128))
        state[1] = jnp.broadcast_to(curve, (8, 128))
        return carry

    lax.fori_loop(0, 2, iteration, 0)


def last(steps, rs, kept_in, image_in, sol_out, res_out, kept_out):
    first, second = steps[0, 0:1, 0:1], steps[1, 0:1, 0:1]
    first = first - second * steps[3, 0:1, 0:1]
    sol_out[0] = first * kept_in[0, 0] + second * kept_in[1, 0]
    res_out[0] = rs[0] - (first * image_in[0, 0] + second * image_in[1, 0])
    kept_out[...] = kept_in[...]


def local(right_side, permeability, lift_weight, spectral_weight, mix_weight, proj_weight):
    smem = pl.BlockSpec(memory_space=pltpu.SMEM)
    hbm = pl.BlockSpec(memory_space=pl.ANY)
    field = (LX, LY, NZ)
    dma = pltpu.SemaphoreType.DMA
    scratch = [
        pltpu.VMEM(field, F32),
        pltpu.VMEM(field, BF16),
        pltpu.VMEM((CH, CH + 1), F32),
        pltpu.VMEM((2, 2, CH, CH, 64), F32),
        pltpu.VMEM((LX * NZ, 256), BF16),
        pltpu.VMEM((LX, 768, NZ), BF16),
        pltpu.VMEM((128, 256), BF16),
        pltpu.VMEM((256, 192), BF16),
        pltpu.VMEM((512, 128), BF16),
        pltpu.VMEM((128, 512), BF16),
        pltpu.VMEM((32, 128), BF16),
        pltpu.VMEM((128, 16), BF16),
        pltpu.VMEM((16, 256), BF16),
        pltpu.VMEM((64, CH, 16, NZ), BF16),
        pltpu.VMEM((LX, 16, CH, 8, NZ), F32),
        pltpu.VMEM(field, F32),
        pltpu.VMEM((LX + 2, LY + 16, NZ), F32),
        pltpu.VMEM((LX + 2, LY + 16, NZ), F32),
        pltpu.VMEM((6,) + field, F32),
        pltpu.VMEM(field, F32),
        pltpu.VMEM(field, F32),
        pltpu.VMEM(field, F32),
        pltpu.VMEM((256, 256), BF16),
        pltpu.VMEM((128, 256), BF16),
        pltpu.VMEM((256, 192), BF16),
        pltpu.VMEM((LY, NZ), BF16),
        pltpu.VMEM((LY, NZ), BF16),
        pltpu.VMEM((LX, 16, NZ), BF16),
        pltpu.VMEM((LX, 16, NZ), BF16),
        pltpu.VMEM((4, NR, 16, 128), F32),
        pltpu.VMEM((4, NR, 16, 128), F32),
        pltpu.VMEM((4, NC, 8, 128), F32),
        pltpu.VMEM((4, NC, 8, 128), F32),
        pltpu.VMEM((4, 8, 128), F32),
        pltpu.VMEM((NC, 4, 8, 128), F32),
        pltpu.VMEM((4, NR, 16, 128), F32),
        pltpu.VMEM((4, NR, 16, 128), F32),
        pltpu.VMEM((CH, LY, 768), BF16),
        pltpu.VMEM((3, 8, 128), F32),
        pltpu.VMEM((3, NC, 8, 128), F32),
        pltpu.VMEM((3, 8, 128), F32),
        pltpu.VMEM((3, NR, 8, 128), F32),
        pltpu.VMEM((2, 8, 128), F32),
        dma((4,)), dma((4,)), dma((4,)), dma((4,)), dma((4,)), dma((4,)),
        dma((4,)), dma((4,)), dma, dma, dma((4,)), dma((4,)),
        dma((3,)), dma((3,)), dma((3,)), dma((3,)), dma((15,)), dma, dma,
    ]
    constants = [jnp.asarray(t) for t in tables()]
    pair = jax.ShapeDtypeStruct((2,) + field, F32)
    kept, images, steps = pl.pallas_call(
        kernel,
        out_shape=[pair, pair, jax.ShapeDtypeStruct((4, 8, 128), F32)],
        in_specs=[hbm, hbm, smem, smem, smem] + [hbm] * 13,
        out_specs=[hbm, hbm, pl.BlockSpec(memory_space=pltpu.VMEM)],
        scratch_shapes=scratch,
        compiler_params=pltpu.CompilerParams(
            collective_id=0, has_side_effects=True, vmem_limit_bytes=56 * 1024 * 1024
        ),
    )(
        right_side, permeability, lift_weight.T, mix_weight, proj_weight, mix_weight,
        spectral_weight, *constants,
    )
    plane = (1, LY, NZ)
    one = pl.BlockSpec(plane, lambda x: (x, 0, 0))
    two = pl.BlockSpec((2,) + plane, lambda x: (0, x, 0, 0))
    return pl.pallas_call(
        last,
        grid=(LX,),
        out_shape=[jax.ShapeDtypeStruct(field, F32), jax.ShapeDtypeStruct(field, F32), pair],
        in_specs=[pl.BlockSpec((4, 8, 128), lambda x: (0, 0, 0)), one, two, two],
        out_specs=[one, one, two],
    )(steps, right_side, kept, images)


def solution(mesh):
    placed = (
        P("row", "col", None), P("row", "col", None), P(), P(None, "row", None, None, "col"), P(), P(),
    )
    return jax.shard_map(
        local,
        mesh=mesh,
        in_specs=placed,
        out_specs=(P("row", "col", None), P("row", "col", None), P(None, "row", "col", None)),
        check_vma=False,
    )
```

```python
import jax
import jax.numpy as jnp
import ml_dtypes
import numpy as np
from jax import lax
from jax.experimental import pallas as pl
from jax.experimental.pallas import tpu as pltpu
from jax.sharding import PartitionSpec as P

F32 = jnp.float32
BF16 = jnp.bfloat16
MESH = pl.DeviceIdType.MESH
NR, NC = 16, 8
NX, NY, NZ = 64, 1024, 256
LX, LY = NX // NR, NY // NC
CH = 16
CELLS = float(NX * NY * NZ)
GELU_A = float(np.sqrt(2.0 / np.pi))


def pieces(table):
    high = table.astype(ml_dtypes.bfloat16)
    low = (table - high.astype(np.float64)).astype(ml_dtypes.bfloat16)
    return high, low


def waves(freqs, places, length):
    angle = 2.0 * np.pi * ((freqs[None, :] * places[:, None]) % length) / length
    return np.cos(angle), np.sin(angle)


def tables():
    cz, sz = waves(np.arange(32), np.arange(NZ), NZ)
    tz = np.zeros((LX, NZ, 2, 32, LX))
    ti = np.zeros((2, 32, LX, LX, NZ))
    for x in range(LX):
        tz[x, :, 0, :, x] = cz
        tz[x, :, 1, :, x] = sz
        ti[0, :, x, x, :] = cz.T
        ti[1, :, x, x, :] = -sz.T
    tz = pieces(tz.reshape(LX * NZ, 256))[0]
    ti_high, ti_low = pieces(ti.reshape(256, LX * NZ))
    ti = np.concatenate([ti_high, ti_high, ti_low], axis=0)
    ti = np.ascontiguousarray(ti.reshape(768, LX, NZ).transpose(1, 0, 2))

    yt = np.zeros((NC, 2, 32, 2, LY))
    yi = np.zeros((NC, 2, LY, 2, 32))
    for col in range(NC):
        cy, sy = waves(np.arange(-16, 16), np.arange(LY) + col * LY, NY)
        yt[col, 0, :, 0] = cy.T
        yt[col, 0, :, 1] = -sy.T
        yt[col, 1, :, 0] = -sy.T
        yt[col, 1, :, 1] = -cy.T
        yi[col, 0, :, 0] = cy
        yi[col, 0, :, 1] = -sy
        yi[col, 1, :, 0] = sy
        yi[col, 1, :, 1] = cy
    yt = np.concatenate(pieces(yt.reshape(NC, 64, 256)), axis=1)
    yi_high, yi_low = pieces(yi.reshape(NC, 256, 64))
    yi = np.concatenate([yi_high, yi_high, yi_low], axis=2)

    cx, sx = waves(np.arange(-8, 8), np.arange(NX), NX)
    cx = cx.reshape(NR, LX, NC, 2)
    sx = sx.reshape(NR, LX, NC, 2)
    xt = np.zeros((NC, 2, 2, 2, NR, 2, 2, LX))
    xi = np.zeros((NR, 2, 2, LX, NC, 2, 2, 2))
    for kz in range(2):
        forward_cos = cx.transpose(2, 3, 0, 1)
        forward_sin = sx.transpose(2, 3, 0, 1)
        xt[:, kz, :, 0, :, 0, kz, :] = forward_cos
        xt[:, kz, :, 0, :, 1, kz, :] = forward_sin
        xt[:, kz, :, 1, :, 1, kz, :] = forward_cos
        xt[:, kz, :, 1, :, 0, kz, :] = -forward_sin
        xi[:, 0, kz, :, :, kz, :, 0] = cx
        xi[:, 0, kz, :, :, kz, :, 1] = -sx
        xi[:, 1, kz, :, :, kz, :, 1] = cx
        xi[:, 1, kz, :, :, kz, :, 0] = sx
    xt = np.concatenate(pieces(xt.reshape(64, 256)), axis=0)
    xi_high, xi_low = pieces(xi.reshape(256, 64) * (0.5 / CELLS))
    xi = np.concatenate([xi_high, xi_high, xi_low], axis=1)

    fold = np.zeros((4, 4, 32, 4, 32))
    for r in range(4):
        for c in range(4):
            fold[r, c, :, r, :] = np.eye(32)
    fold = fold.reshape(512, 128)
    spread = np.ascontiguousarray(fold.T)
    gather = np.zeros((4, 4, 2, 4, 2, 16))
    for quad in range(4):
        for r in range(4):
            for ri in range(2):
                gather[quad, r, ri, r, ri, quad * 4 : quad * 4 + 4] = 1.0
    gather = gather.reshape(32, 128)
    left = np.kron(np.eye(16), np.ones((8, 1)))
    right = np.zeros((16, 16, 2, 8))
    for c in range(16):
        right[c, c] = 1.0
    right = right.reshape(16, 256)
    b16 = lambda a: a.astype(ml_dtypes.bfloat16)
    return tz, ti, yt, yi, xt, xi, b16(fold), b16(spread), b16(gather), b16(left), b16(right)


def split(value):
    high = value.astype(BF16)
    return high, (value - high.astype(F32)).astype(BF16)


def dot(left, right):
    return jnp.dot(left, right, preferred_element_type=F32)


def kernel(
    rs, perm_in, lw, mw, pw, mix_in, weight_in,
    tz_in, ti_in, yt_all, yi_all, xt_in, xi_in, fold_in, spread_in, gather_in, left_in, right_in,
    kept_out, image_out, steps_out,
    res, perm, mixv, weight, tz, ti, xt, xi, fold, spread, gather, left_map, right_map,
    lift, point, logp, padk, padp, faces, prev, image, fresh, maps, yt, yi,
    plx, phx, ply, phy,
    sf, vf, sx, vx, sm, vm, sh, vh, modes,
    asrc, aall, state,
    perm_s, perm_r, halo_s, halo_r, f_s, f_r, x_s, x_r, m_s, m_r, h_s, h_r, ac_s, ac_r, table_s, kept_s, image_s,
):
    row = lax.axis_index("row")
    col = lax.axis_index("col")
    up_row, down_row = lax.rem(row + 1, NR), lax.rem(row + NR - 1, NR)
    up_col, down_col = lax.rem(col + 1, NC), lax.rem(col + NC - 1, NC)

    def send(src, dst, s, r, to_row, to_col):
        return pltpu.make_async_remote_copy(
            src_ref=src, dst_ref=dst, send_sem=s, recv_sem=r, device_id=(to_row, to_col), device_id_type=MESH
        )

    loads = [
        (rs, res), (perm_in, perm), (mix_in, mixv), (left_in, left_map), (right_in, right_map), (tz_in, tz),
        (yt_all.at[col], yt), (xt_in, xt), (weight_in, weight), (fold_in, fold), (spread_in, spread),
        (gather_in, gather), (xi_in, xi), (yi_all.at[col], yi), (ti_in, ti),
    ]
    loads = [pltpu.make_async_copy(src, dst, table_s.at[n]) for n, (src, dst) in enumerate(loads)]
    for copy in loads:
        copy.start()

    barrier = pltpu.get_barrier_semaphore()

    def to_all(act):
        for other in range(1, NC):
            act(row, lax.rem(col + other, NC))

        def step(k, carry):
            to_row = lax.rem(row + k, NR)
            for other in range(NC):
                act(to_row, lax.rem(col + other, NC))
            return carry

        lax.fori_loop(1, NR, step, 0)

    to_all(lambda r, c: pl.semaphore_signal(barrier, 1, device_id=(r, c), device_id_type=MESH))
    pl.semaphore_wait(barrier, NR * NC - 1)

    perm_copies = [
        send(perm_in.at[LX - 1], plx, perm_s.at[0], perm_r.at[0], up_row, col),
        send(perm_in.at[0], phx, perm_s.at[1], perm_r.at[1], down_row, col),
        send(perm_in.at[:, pl.ds(LY - 16, 16), :], ply, perm_s.at[2], perm_r.at[2], row, up_col),
        send(perm_in.at[:, pl.ds(0, 16), :], phy, perm_s.at[3], perm_r.at[3], row, down_col),
    ]
    for copy in perm_copies:
        copy.start()

    def sums_begin(u, line):
        me = row * NC + col
        asrc[u] = line
        aall[u, me] = line
        to_all(lambda r, c: send(asrc.at[u], aall.at[u, me], ac_s.at[u], ac_r.at[u], r, c).start())

    def sums_end(u):
        whole = send(
            aall.at[u, pl.ds(0, NR * NC - 1)], aall.at[u, pl.ds(0, NR * NC - 1)], ac_s.at[u], ac_r.at[u], row, col
        )
        whole.wait_recv()
        whole.wait_send()
        return jnp.sum(aall[u], axis=0)

    def tile_of(parts):
        rows = []
        for part in parts:
            line = jnp.sum(part, axis=0, keepdims=True)
            rows.append(line[:, :128] + line[:, 128:])
        index = lax.broadcasted_iota(jnp.int32, (8, 128), 0)
        tile = jnp.zeros((8, 128), F32)
        for i, line in enumerate(rows):
            tile = jnp.where(index == i, jnp.broadcast_to(line, (8, 128)), tile)
        each = jnp.broadcast_to(jnp.sum(tile, axis=1, keepdims=True), (8, 128))
        lane = lax.broadcasted_iota(jnp.int32, (8, 128), 1)
        return jnp.sum(jnp.where(index == lane, each, 0.0), axis=0, keepdims=True)

    def first_pass(b, total):
        x, y = lax.div(b, 4), pl.multiple_of(lax.rem(b, 4) * 32, 32)
        value = res[x, pl.ds(y, 32), :]
        squares = value * value
        return total + (squares[0:8] + squares[8:16]) + (squares[16:24] + squares[24:32])

    loads[0].wait()
    total = lax.fori_loop(0, 16, first_pass, jnp.zeros((8, NZ), F32))
    sums_begin(0, tile_of([total]))

    def second_pass(b, carry):
        x, y = lax.div(b, 4), pl.multiple_of(lax.rem(b, 4) * 32, 32)
        value = perm[x, pl.ds(y, 32), :].astype(F32)
        padp[x + 1, pl.ds(pl.multiple_of(y + 8, 8), 32), :] = value
        logp[x, pl.ds(y, 32), :] = jnp.log(value)
        zero = jnp.zeros((32, NZ), F32)
        prev[x, pl.ds(y, 32), :] = zero
        image[x, pl.ds(y, 32), :] = zero
        return carry

    for copy in loads[1:5]:
        copy.wait()
    lax.fori_loop(0, 16, second_pass, 0)
    mix_high, mix_low = split(mixv[:, 0:CH] * 0.5)
    rows_iota = lax.broadcasted_iota(jnp.int32, (128, 256), 0)
    lane_iota = lax.broadcasted_iota(jnp.int32, (128, 256), 1)
    same = lax.rem(rows_iota, 8) == lax.rem(lane_iota, 8)
    for n, piece in enumerate((mix_high, mix_low)):
        wide = dot(left_map[...], dot(piece, right_map[...]).astype(BF16))
        maps[n * 128 : (n + 1) * 128, :] = jnp.where(same, wide, 0.0).astype(BF16)

    lanes = lax.broadcasted_iota(jnp.int32, (32, NZ), 1)

    def around(ref, x, y, edge):
        own = ref[x + 1, pl.ds(y, 48), :]
        here = own[8:40]
        before = pltpu.roll(here, 1, 1)
        after = pltpu.roll(here, NZ - 1, 1)
        if edge:
            before = jnp.where(lanes == 0, here, before)
            after = jnp.where(lanes == NZ - 1, here, after)
        else:
            before = jnp.where(lanes == 0, 0.0, before)
            after = jnp.where(lanes == NZ - 1, 0.0, after)
        return here, (
            ref[x, pl.ds(pl.multiple_of(y + 8, 8), 32), :], ref[x + 2, pl.ds(pl.multiple_of(y + 8, 8), 32), :], own[7:39], own[9:41], before, after
        )

    def build_faces():
        for copy in perm_copies:
            copy.wait()
        padp[0, pl.ds(8, LY), :] = plx[...].astype(F32)
        padp[LX + 1, pl.ds(8, LY), :] = phx[...].astype(F32)
        for x in range(LX):
            padp[x + 1, pl.ds(0, 8), :] = ply[x].astype(F32)[8:16]
            padp[x + 1, pl.ds(LY + 8, 8), :] = phy[x].astype(F32)[0:8]

        @pl.when(row == 0)
        def _():
            padp[0, pl.ds(8, LY), :] = padp[1, pl.ds(8, LY), :]

        @pl.when(row == NR - 1)
        def _():
            padp[LX + 1, pl.ds(8, LY), :] = padp[LX, pl.ds(8, LY), :]

        @pl.when(col == 0)
        def _():
            for x in range(LX):
                padp[x + 1, pl.ds(0, 8), :] = jnp.broadcast_to(padp[x + 1, pl.ds(8, 8), :][0:1], (8, NZ))

        @pl.when(col == NC - 1)
        def _():
            for x in range(LX):
                padp[x + 1, pl.ds(LY + 8, 8), :] = jnp.broadcast_to(padp[x + 1, pl.ds(LY, 8), :][7:8], (8, NZ))

        def face_pass(b, carry):
            x, y = lax.div(b, 4), pl.multiple_of(lax.rem(b, 4) * 32, 32)
            here, others = around(padp, x, y, True)
            for n, other in enumerate(others):
                faces[n, x, pl.ds(y, 32), :] = 2.0 * here * other / (here + other)
            return carry

        lax.fori_loop(0, 16, face_pass, 0)

    for copy in loads[5:]:
        copy.wait()
    state[0] = jnp.broadcast_to(sums_end(0)[:, 0:1], (8, 128))
    state[1] = jnp.ones((8, 128), F32)

    mask_rows = lax.broadcasted_iota(jnp.int32, (16, 128), 0)
    mask_lanes = lax.broadcasted_iota(jnp.int32, (16, 128), 1)
    quad_mask = lax.rem(mask_rows, 4) == mask_lanes // 32
    low_half = lax.broadcasted_iota(jnp.int32, (8, 128), 0) < 4

    def iteration(i, carry):
        mean = state[0][0:1, 0:1] * (1.0 / CELLS) + 1e-6
        scale = jnp.sqrt(mean)
        inverse = 1.0 / scale

        def along_x(cq):
            whole = send(
                sf.at[cq, pl.ds(0, NR - 1)], vf.at[cq, pl.ds(0, NR - 1)], f_s.at[cq], f_r.at[cq], row, col
            )
            whole.wait_recv()
            whole.wait_send()
            high, low = split(vf[cq].reshape(256, 128))
            both = dot(xt[...], high)
            sx[cq] = (both[:64] + both[64:] + dot(xt[0:64, :], low)).reshape(NC, 8, 128)
            vx[cq, col] = sx[cq, col]

            def scatter(k, carry):
                to = lax.rem(col + k, NC)
                send(sx.at[cq, to], vx.at[cq, col], x_s.at[cq], x_r.at[cq], row, to).start()
                return carry

            lax.fori_loop(1, NC, scatter, 0, unroll=True)

        def forward(cq, carry):
            def lift_pass(b, carry):
                x, y = lax.div(b, 16), pl.multiple_of(lax.rem(b, 16) * 8, 8)
                scaled = res[x, pl.ds(y, 8), :] * inverse
                logs = logp[x, pl.ds(y, 8), :]
                for c4 in range(4):
                    c = cq * 4 + c4
                    half = (lw[0, c] * 0.5) * scaled + (lw[1, c] * 0.5) * logs + lw[2, c] * 0.5
                    inner = half * (2.0 * GELU_A + (8.0 * 0.044715 * GELU_A) * (half * half))
                    value = half + half * jnp.tanh(inner)
                    rest = value - value.astype(BF16).astype(F32)
                    lift[b, c] = jnp.concatenate([value, rest], axis=0).astype(BF16)
                return carry

            lax.fori_loop(0, 64, lift_pass, 0, unroll=8)
            tops, bottoms = [], []
            for c4 in range(4):
                c = cq * 4 + c4
                block = jnp.concatenate(
                    [lift[x * 16 : x * 16 + 16, c].reshape(256, NZ) for x in range(LX)], axis=1
                )
                deep = dot(block, tz[...]).reshape(16, 2, 8, 256)
                deep = (deep[:, 0] + deep[:, 1]).reshape(128, 256)
                tops.append(deep[:, :128])
                bottoms.append(deep[:, 128:])
            high, low = split(
                jnp.concatenate([jnp.concatenate(tops, axis=1), jnp.concatenate(bottoms, axis=1)], axis=0)
            )
            both = dot(yt[...], high)
            flat = both[:64] + both[64:] + dot(yt[0:64, :], low)
            turned = []
            for ri in range(2):
                square = jnp.concatenate(
                    [flat[ri * 32 : ri * 32 + 32, c4 * 128 : c4 * 128 + 128] for c4 in range(4)], axis=0
                )
                turned.append(square.T.reshape(NR, 8, 128))
            sf[cq] = jnp.concatenate(turned, axis=1)
            vf[cq, row] = sf[cq, row]

            def step(k, carry):
                to = lax.rem(row + k, NR)
                send(sf.at[cq, to], vf.at[cq, row], f_s.at[cq], f_r.at[cq], to, col).start()
                return carry

            lax.fori_loop(1, NR, step, 0, unroll=True)

            return carry

        lax.fori_loop(0, 4, forward, 0)
        def point_pass(b, carry):
            x, y = lax.div(b, 16), lax.rem(b, 16)
            both = dot(maps[...], lift[b].reshape(256, NZ))
            point[x, y] = (both[:128] + both[128:]).reshape(CH, 8, NZ)
            return carry

        along_x(0)
        along_x(1)
        lax.fori_loop(0, 40, point_pass, 0, unroll=8)
        along_x(2)
        along_x(3)
        lax.fori_loop(40, 64, point_pass, 0, unroll=8)

        @pl.when(i == 0)
        def _():
            build_faces()


        spectrum = []
        for cq in range(4):
            whole = send(
                sx.at[cq, pl.ds(0, NC - 1)], vx.at[cq, pl.ds(0, NC - 1)], x_s.at[cq], x_r.at[cq], row, col
            )
            whole.wait_recv()
            whole.wait_send()
            spectrum.append(jnp.sum(vx[cq], axis=0))

        stacks = []
        for ri in range(2):
            tiles = []
            for r in range(4):
                line = r * 2 + ri
                wide = [
                    jnp.broadcast_to(spectrum[q][line : line + 1], (8, 128)) for q in range(4)
                ]
                tall = jnp.concatenate(
                    [jnp.where(low_half, wide[0], wide[1]), jnp.where(low_half, wide[2], wide[3])], axis=0
                )
                tiles.append(jnp.where(quad_mask, tall, 0.0))
            stacks.append(jnp.concatenate(tiles, axis=1))
        high, low = split(jnp.concatenate(stacks, axis=0))
        both = dot(jnp.concatenate([high, low], axis=0), fold[...])
        ordered = both[:32] + both[32:]

        reals, imags = [], []
        for kz in range(2):
            real = jnp.zeros((CH, 64), F32)
            imag = jnp.zeros((CH, 64), F32)
            for c in range(CH):
                value_real = ordered[c : c + 1, kz * 64 : kz * 64 + 64]
                value_imag = ordered[CH + c : CH + c + 1, kz * 64 : kz * 64 + 64]
                weight_real = weight[0, kz, c]
                weight_imag = weight[1, kz, c]
                real = real + (weight_real * value_real - weight_imag * value_imag)
                imag = imag + (weight_real * value_imag + weight_imag * value_real)
            reals.append(real)
            imags.append(imag)
        mixed = jnp.concatenate([jnp.concatenate(reals, axis=1), jnp.concatenate(imags, axis=1)], axis=0)

        high, low = split(mixed)
        both = dot(jnp.concatenate([high, low], axis=0), spread[...])
        wide = both[:32] + both[32:]
        mask = jnp.concatenate([quad_mask, quad_mask], axis=0)
        tall = jnp.concatenate(
            [jnp.where(mask, wide[:, r * 128 : r * 128 + 128], 0.0) for r in range(4)], axis=0
        )
        high, low = split(tall)
        both = dot(gather[...], jnp.concatenate([high, low], axis=1))
        sm[...] = (both[:, :128] + both[:, 128:]).reshape(4, 8, 128)
        vm[col] = sm[...]

        def spread_out(k, carry):
            send(sm, vm.at[col], m_s, m_r, row, lax.rem(col + k, NC)).start()
            return carry

        lax.fori_loop(1, NC, spread_out, 0, unroll=True)
        whole = send(vm.at[pl.ds(0, NC - 1)], vm.at[pl.ds(0, NC - 1)], m_s, m_r, row, col)
        whole.wait_recv()
        whole.wait_send()

        high, low = split(jnp.concatenate([vm[:, oq].reshape(64, 128) for oq in range(4)], axis=1))
        back = dot(xi[...], jnp.concatenate([high, low, high], axis=0))
        for oq in range(4):
            sh[oq] = back[:, oq * 128 : oq * 128 + 128].reshape(NR, 16, 128)
            vh[oq, row] = sh[oq, row]

            def step(k, carry, oq=oq):
                to = lax.rem(row + k, NR)
                send(sh.at[oq, to], vh.at[oq, row], h_s.at[oq], h_r.at[oq], to, col).start()
                return carry

            lax.fori_loop(1, NR, step, 0, unroll=True)

        def clear(b, carry):
            x, y = lax.div(b, 4), pl.multiple_of(lax.rem(b, 4) * 32, 32)
            padk[x + 1, pl.ds(pl.multiple_of(y + 8, 8), 32), :] = jnp.full((32, NZ), pw[CH], F32)
            return carry

        lax.fori_loop(0, 16, clear, 0)

        def turn(oq):
            whole = send(
                sh.at[oq, pl.ds(0, NR - 1)], vh.at[oq, pl.ds(0, NR - 1)], h_s.at[oq], h_r.at[oq], row, col
            )
            whole.wait_recv()
            whole.wait_send()
            turned = [vh[oq, :, pl.ds(ri * 8, 8), :].reshape(128, 128).T for ri in range(2)]
            block = jnp.concatenate(
                [
                    jnp.concatenate([turned[ri][o4 * 32 : o4 * 32 + 32] for ri in range(2)], axis=0)
                    for o4 in range(4)
                ],
                axis=1,
            )
            high, low = split(block)
            back = dot(yi[...], jnp.concatenate([high, low, high], axis=0))
            for o4 in range(4):
                part = back[:, o4 * 128 : o4 * 128 + 128]
                high, low = split(jnp.concatenate([part[:128], part[128:]], axis=1))
                modes[o4] = jnp.concatenate([high, low, high], axis=1)

        def channels(oq, xs):
            for x in xs:
                for o4 in range(4):
                    o = oq * 4 + o4
                    bias = mw[o, CH] * 0.5
                    wave = dot(modes[o4], ti[x])
                    half = wave + point[x, :, o].reshape(LY, NZ) + bias
                    inner = half * (2.0 * GELU_A + (8.0 * 0.044715 * GELU_A) * (half * half))
                    hidden = pw[o] * (half + half * jnp.tanh(inner))
                    padk[x + 1, pl.ds(8, LY), :] += hidden

        def backward(oq, carry):
            turn(oq)
            channels(oq, range(LX))
            return carry

        def planes(xs):
            channels(3, xs)
            for x in xs:
                padk[x + 1, pl.ds(8, LY), :] = scale * padk[x + 1, pl.ds(8, LY), :]

        lax.fori_loop(0, 3, backward, 0)
        turn(3)
        planes((0, LX - 1))
        copies = [
            send(padk.at[LX, pl.ds(8, LY)], padk.at[0, pl.ds(8, LY)], halo_s.at[0], halo_r.at[0], up_row, col),
            send(padk.at[1, pl.ds(8, LY)], padk.at[LX + 1, pl.ds(8, LY)], halo_s.at[1], halo_r.at[1], down_row, col),
            send(
                padk.at[pl.ds(1, LX), pl.ds(LY, 8)], padk.at[pl.ds(1, LX), pl.ds(0, 8)],
                halo_s.at[2], halo_r.at[2], row, up_col,
            ),
            send(
                padk.at[pl.ds(1, LX), pl.ds(8, 8)], padk.at[pl.ds(1, LX), pl.ds(LY + 8, 8)],
                halo_s.at[3], halo_r.at[3], row, down_col,
            ),
        ]
        for copy in copies[:2]:
            copy.start()
        planes(range(1, LX - 1))
        for copy in copies[2:]:
            copy.start()
        keep = pltpu.make_async_copy(padk.at[pl.ds(1, LX), pl.ds(8, LY)], kept_out.at[i], kept_s)
        keep.start()
        for copy in copies:
            copy.wait()

        @pl.when(row == 0)
        def _():
            padk[0, pl.ds(8, LY), :] = jnp.zeros((LY, NZ), F32)

        @pl.when(row == NR - 1)
        def _():
            padk[LX + 1, pl.ds(8, LY), :] = jnp.zeros((LY, NZ), F32)

        @pl.when(col == 0)
        def _():
            padk[pl.ds(1, LX), pl.ds(0, 8), :] = jnp.zeros((LX, 8, NZ), F32)

        @pl.when(col == NC - 1)
        def _():
            padk[pl.ds(1, LX), pl.ds(LY + 8, 8), :] = jnp.zeros((LX, 8, NZ), F32)

        def fold8(value):
            return (value[0:8] + value[8:16]) + (value[16:24] + value[24:32])

        def operator_pass(b, totals):
            x, y = lax.div(b, 4), pl.multiple_of(lax.rem(b, 4) * 32, 32)
            here, others = around(padk, x, y, False)
            applied = jnp.zeros((32, NZ), F32)
            for n, other in enumerate(others):
                applied = applied + faces[n, x, pl.ds(y, 32), :] * (here - other)
            fresh[x, pl.ds(y, 32), :] = applied
            old_image = image[x, pl.ds(y, 32), :]
            residual = res[x, pl.ds(y, 32), :]
            old = prev[x, pl.ds(y, 32), :]
            terms = (
                here * applied, here * old_image, residual * here, residual * old, residual * applied,
                applied * applied,
            )
            return tuple(total + fold8(term) for total, term in zip(totals, terms))

        totals = lax.fori_loop(0, 16, operator_pass, tuple(jnp.zeros((8, NZ), F32) for _ in range(6)))
        sums_begin(1 + i, tile_of(totals))
        sums = sums_end(1 + i)
        k_ak, k_img, r_k, r_d, r_ak, ak_ak = [sums[:, n : n + 1] for n in range(6)]
        old_curve = state[1][0:1, 0:1]
        beta = k_img / old_curve
        curve = k_ak - 2.0 * beta * k_img + beta * beta * old_curve
        alpha = (r_k - beta * r_d) / curve

        show = pltpu.make_async_copy(fresh, image_out.at[i], image_s)
        show.start()

        @pl.when(i == 0)
        def _():
            def update(b, carry):
                x, y = lax.div(b, 4), pl.multiple_of(lax.rem(b, 4) * 32, 32)
                at = (x, pl.ds(y, 32), slice(None))
                applied = fresh[at]
                prev[at] = padk[x + 1, pl.ds(pl.multiple_of(y + 8, 8), 32), :]
                image[at] = applied
                res[at] = res[at] - alpha * applied
                return carry

            lax.fori_loop(0, 16, update, 0)

        steps_out[i] = jnp.broadcast_to(alpha, (8, 128))
        steps_out[2 + i] = jnp.broadcast_to(beta, (8, 128))
        keep.wait()
        show.wait()
        squares = state[0][0:1, 0:1] - 2.0 * alpha * r_ak + alpha * alpha * ak_ak
        state[0] = jnp.broadcast_to(jnp.maximum(squares, 0.0), (8, 128))
        state[1] = jnp.broadcast_to(curve, (8, 128))
        return carry

    lax.fori_loop(0, 2, iteration, 0)


def last(steps, rs, kept_in, image_in, sol_out, res_out, kept_out):
    first, second = steps[0, 0:1, 0:1], steps[1, 0:1, 0:1]
    first = first - second * steps[3, 0:1, 0:1]
    sol_out[...] = first * kept_in[0] + second * kept_in[1]
    res_out[...] = rs[...] - (first * image_in[0] + second * image_in[1])
    kept_out[...] = kept_in[...]


def local(right_side, permeability, lift_weight, spectral_weight, mix_weight, proj_weight):
    smem = pl.BlockSpec(memory_space=pltpu.SMEM)
    hbm = pl.BlockSpec(memory_space=pl.ANY)
    field = (LX, LY, NZ)
    dma = pltpu.SemaphoreType.DMA
    scratch = [
        pltpu.VMEM(field, F32),
        pltpu.VMEM(field, BF16),
        pltpu.VMEM((CH, CH + 1), F32),
        pltpu.VMEM((2, 2, CH, CH, 64), F32),
        pltpu.VMEM((LX * NZ, 256), BF16),
        pltpu.VMEM((LX, 768, NZ), BF16),
        pltpu.VMEM((128, 256), BF16),
        pltpu.VMEM((256, 192), BF16),
        pltpu.VMEM((512, 128), BF16),
        pltpu.VMEM((128, 512), BF16),
        pltpu.VMEM((32, 128), BF16),
        pltpu.VMEM((128, 16), BF16),
        pltpu.VMEM((16, 256), BF16),
        pltpu.VMEM((64, CH, 16, NZ), BF16),
        pltpu.VMEM((LX, 16, CH, 8, NZ), F32),
        pltpu.VMEM(field, F32),
        pltpu.VMEM((LX + 2, LY + 16, NZ), F32),
        pltpu.VMEM((LX + 2, LY + 16, NZ), F32),
        pltpu.VMEM((6,) + field, F32),
        pltpu.VMEM(field, F32),
        pltpu.VMEM(field, F32),
        pltpu.VMEM(field, F32),
        pltpu.VMEM((256, 256), BF16),
        pltpu.VMEM((128, 256), BF16),
        pltpu.VMEM((256, 192), BF16),
        pltpu.VMEM((LY, NZ), BF16),
        pltpu.VMEM((LY, NZ), BF16),
        pltpu.VMEM((LX, 16, NZ), BF16),
        pltpu.VMEM((LX, 16, NZ), BF16),
        pltpu.VMEM((4, NR, 16, 128), F32),
        pltpu.VMEM((4, NR, 16, 128), F32),
        pltpu.VMEM((4, NC, 8, 128), F32),
        pltpu.VMEM((4, NC, 8, 128), F32),
        pltpu.VMEM((4, 8, 128), F32),
        pltpu.VMEM((NC, 4, 8, 128), F32),
        pltpu.VMEM((4, NR, 16, 128), F32),
        pltpu.VMEM((4, NR, 16, 128), F32),
        pltpu.VMEM((4, LY, 768), BF16),
        pltpu.VMEM((3, 1, 128), F32),
        pltpu.VMEM((3, NR * NC, 1, 128), F32),
        pltpu.VMEM((2, 8, 128), F32),
        dma((4,)), dma((4,)), dma((4,)), dma((4,)), dma((4,)), dma((4,)),
        dma((4,)), dma((4,)), dma, dma, dma((4,)), dma((4,)),
        dma((3,)), dma((3,)), dma((15,)), dma, dma,
    ]
    constants = [jnp.asarray(t) for t in tables()]
    pair = jax.ShapeDtypeStruct((2,) + field, F32)
    kept, images, steps = pl.pallas_call(
        kernel,
        out_shape=[pair, pair, jax.ShapeDtypeStruct((4, 8, 128), F32)],
        in_specs=[hbm, hbm, smem, smem, smem] + [hbm] * 13,
        out_specs=[hbm, hbm, pl.BlockSpec(memory_space=pltpu.VMEM)],
        scratch_shapes=scratch,
        compiler_params=pltpu.CompilerParams(
            collective_id=0, has_side_effects=True, vmem_limit_bytes=56 * 1024 * 1024
        ),
    )(
        right_side, permeability, lift_weight.T, mix_weight, proj_weight, mix_weight,
        spectral_weight, *constants,
    )
    plane = (2, LY, NZ)
    one = pl.BlockSpec(plane, lambda x: (x, 0, 0))
    two = pl.BlockSpec((2,) + plane, lambda x: (0, x, 0, 0))
    return pl.pallas_call(
        last,
        grid=(LX // 2,),
        out_shape=[jax.ShapeDtypeStruct(field, F32), jax.ShapeDtypeStruct(field, F32), pair],
        in_specs=[pl.BlockSpec((4, 8, 128), lambda x: (0, 0, 0)), one, two, two],
        out_specs=[one, one, two],
    )(steps, right_side, kept, images)


def solution(mesh):
    placed = (
        P("row", "col", None), P("row", "col", None), P(), P(None, "row", None, None, "col"), P(), P(),
    )
    return jax.shard_map(
        local,
        mesh=mesh,
        in_specs=placed,
        out_specs=(P("row", "col", None), P("row", "col", None), P(None, "row", "col", None)),
        check_vma=False,
    )
```

```python
import jax
import jax.numpy as jnp
import ml_dtypes
import numpy as np
from jax import lax
from jax.experimental import pallas as pl
from jax.experimental.pallas import tpu as pltpu
from jax.sharding import PartitionSpec as P

F32 = jnp.float32
BF16 = jnp.bfloat16
MESH = pl.DeviceIdType.MESH
NR, NC = 16, 8
NX, NY, NZ = 64, 1024, 256
LX, LY = NX // NR, NY // NC
CH = 16
CELLS = float(NX * NY * NZ)
GELU_A = float(np.sqrt(2.0 / np.pi))


def pieces(table):
    high = table.astype(ml_dtypes.bfloat16)
    low = (table - high.astype(np.float64)).astype(ml_dtypes.bfloat16)
    return high, low


def waves(freqs, places, length):
    angle = 2.0 * np.pi * ((freqs[None, :] * places[:, None]) % length) / length
    return np.cos(angle), np.sin(angle)


def tables():
    cz, sz = waves(np.arange(32), np.arange(NZ), NZ)
    tz = np.zeros((LX, NZ, 2, 32, LX))
    ti = np.zeros((2, 32, LX, LX, NZ))
    for x in range(LX):
        tz[x, :, 0, :, x] = cz
        tz[x, :, 1, :, x] = sz
        ti[0, :, x, x, :] = cz.T
        ti[1, :, x, x, :] = -sz.T
    tz = pieces(tz.reshape(LX * NZ, 256))[0]
    ti_high, ti_low = pieces(ti.reshape(256, LX * NZ))
    ti = np.concatenate([ti_high, ti_high, ti_low], axis=0)
    ti = np.ascontiguousarray(ti.reshape(768, LX, NZ).transpose(1, 0, 2))

    yt = np.zeros((NC, 2, 32, 2, LY))
    yi = np.zeros((NC, 2, LY, 2, 32))
    for col in range(NC):
        cy, sy = waves(np.arange(-16, 16), np.arange(LY) + col * LY, NY)
        yt[col, 0, :, 0] = cy.T
        yt[col, 0, :, 1] = -sy.T
        yt[col, 1, :, 0] = -sy.T
        yt[col, 1, :, 1] = -cy.T
        yi[col, 0, :, 0] = cy
        yi[col, 0, :, 1] = -sy
        yi[col, 1, :, 0] = sy
        yi[col, 1, :, 1] = cy
    yt = np.concatenate(pieces(yt.reshape(NC, 64, 256)), axis=1)
    yi_high, yi_low = pieces(yi.reshape(NC, 256, 64))
    yi = np.concatenate([yi_high, yi_high, yi_low], axis=2)

    cx, sx = waves(np.arange(-8, 8), np.arange(NX), NX)
    cx = cx.reshape(NR, LX, NC, 2)
    sx = sx.reshape(NR, LX, NC, 2)
    xt = np.zeros((NC, 2, 2, 2, NR, 2, 2, LX))
    xi = np.zeros((NR, 2, 2, LX, NC, 2, 2, 2))
    for kz in range(2):
        forward_cos = cx.transpose(2, 3, 0, 1)
        forward_sin = sx.transpose(2, 3, 0, 1)
        xt[:, kz, :, 0, :, 0, kz, :] = forward_cos
        xt[:, kz, :, 0, :, 1, kz, :] = forward_sin
        xt[:, kz, :, 1, :, 1, kz, :] = forward_cos
        xt[:, kz, :, 1, :, 0, kz, :] = -forward_sin
        xi[:, 0, kz, :, :, kz, :, 0] = cx
        xi[:, 0, kz, :, :, kz, :, 1] = -sx
        xi[:, 1, kz, :, :, kz, :, 1] = cx
        xi[:, 1, kz, :, :, kz, :, 0] = sx
    xt = np.concatenate(pieces(xt.reshape(64, 256)), axis=0)
    xi_high, xi_low = pieces(xi.reshape(256, 64) * (0.5 / CELLS))
    xi = np.concatenate([xi_high, xi_high, xi_low], axis=1)

    fold = np.zeros((4, 4, 32, 4, 32))
    for r in range(4):
        for c in range(4):
            fold[r, c, :, r, :] = np.eye(32)
    fold = fold.reshape(512, 128)
    spread = np.ascontiguousarray(fold.T)
    gather = np.zeros((4, 4, 2, 4, 2, 16))
    for quad in range(4):
        for r in range(4):
            for ri in range(2):
                gather[quad, r, ri, r, ri, quad * 4 : quad * 4 + 4] = 1.0
    gather = gather.reshape(32, 128)
    left = np.kron(np.eye(16), np.ones((8, 1)))
    right = np.zeros((16, 16, 2, 8))
    for c in range(16):
        right[c, c] = 1.0
    right = right.reshape(16, 256)
    b16 = lambda a: a.astype(ml_dtypes.bfloat16)
    return tz, ti, yt, yi, xt, xi, b16(fold), b16(spread), b16(gather), b16(left), b16(right)


def split(value):
    high = value.astype(BF16)
    return high, (value - high.astype(F32)).astype(BF16)


def dot(left, right):
    return jnp.dot(left, right, preferred_element_type=F32)


def kernel(
    rs, perm_in, lw, mw, pw, mix_in, weight_in,
    tz_in, ti_in, yt_all, yi_all, xt_in, xi_in, fold_in, spread_in, gather_in, left_in, right_in,
    kept_out, image_out, steps_out,
    res, perm, mixv, weight, tz, ti, xt, xi, fold, spread, gather, left_map, right_map,
    lift, point, logp, padk, padp, faces, prev, image, fresh, maps, yt, yi,
    plx, phx, ply, phy,
    sf, vf, sx, vx, sm, vm, sh, vh, modes,
    asrc, aall, state,
    perm_s, perm_r, halo_s, halo_r, f_s, f_r, x_s, x_r, m_s, m_r, h_s, h_r, ac_s, ac_r, table_s, kept_s, image_s,
):
    row = lax.axis_index("row")
    col = lax.axis_index("col")
    up_row, down_row = lax.rem(row + 1, NR), lax.rem(row + NR - 1, NR)
    up_col, down_col = lax.rem(col + 1, NC), lax.rem(col + NC - 1, NC)

    def send(src, dst, s, r, to_row, to_col):
        return pltpu.make_async_remote_copy(
            src_ref=src, dst_ref=dst, send_sem=s, recv_sem=r, device_id=(to_row, to_col), device_id_type=MESH
        )

    loads = [
        (rs, res), (perm_in, perm), (mix_in, mixv), (left_in, left_map), (right_in, right_map), (tz_in, tz),
        (yt_all.at[col], yt), (xt_in, xt), (weight_in, weight), (fold_in, fold), (spread_in, spread),
        (gather_in, gather), (xi_in, xi), (yi_all.at[col], yi), (ti_in, ti),
    ]
    loads = [pltpu.make_async_copy(src, dst, table_s.at[n]) for n, (src, dst) in enumerate(loads)]
    for copy in loads:
        copy.start()

    barrier = pltpu.get_barrier_semaphore()

    def to_all(act):
        for other in range(1, NC):
            act(row, lax.rem(col + other, NC))

        def step(k, carry):
            to_row = lax.rem(row + k, NR)
            for other in range(NC):
                act(to_row, lax.rem(col + other, NC))
            return carry

        lax.fori_loop(1, NR, step, 0)

    to_all(lambda r, c: pl.semaphore_signal(barrier, 1, device_id=(r, c), device_id_type=MESH))
    pl.semaphore_wait(barrier, NR * NC - 1)

    perm_copies = [
        send(perm_in.at[LX - 1], plx, perm_s.at[0], perm_r.at[0], up_row, col),
        send(perm_in.at[0], phx, perm_s.at[1], perm_r.at[1], down_row, col),
        send(perm_in.at[:, pl.ds(LY - 16, 16), :], ply, perm_s.at[2], perm_r.at[2], row, up_col),
        send(perm_in.at[:, pl.ds(0, 16), :], phy, perm_s.at[3], perm_r.at[3], row, down_col),
    ]
    for copy in perm_copies:
        copy.start()

    def sums_begin(u, line):
        me = row * NC + col
        asrc[u] = line
        aall[u, me] = line
        to_all(lambda r, c: send(asrc.at[u], aall.at[u, me], ac_s.at[u], ac_r.at[u], r, c).start())

    def sums_end(u):
        whole = send(
            aall.at[u, pl.ds(0, NR * NC - 1)], aall.at[u, pl.ds(0, NR * NC - 1)], ac_s.at[u], ac_r.at[u], row, col
        )
        whole.wait_recv()
        whole.wait_send()
        return jnp.sum(aall[u], axis=0)

    def tile_of(parts):
        rows = []
        for part in parts:
            line = jnp.sum(part, axis=0, keepdims=True)
            rows.append(line[:, :128] + line[:, 128:])
        index = lax.broadcasted_iota(jnp.int32, (8, 128), 0)
        tile = jnp.zeros((8, 128), F32)
        for i, line in enumerate(rows):
            tile = jnp.where(index == i, jnp.broadcast_to(line, (8, 128)), tile)
        each = jnp.broadcast_to(jnp.sum(tile, axis=1, keepdims=True), (8, 128))
        lane = lax.broadcasted_iota(jnp.int32, (8, 128), 1)
        return jnp.sum(jnp.where(index == lane, each, 0.0), axis=0, keepdims=True)

    def first_pass(b, total):
        x, y = lax.div(b, 4), pl.multiple_of(lax.rem(b, 4) * 32, 32)
        value = res[x, pl.ds(y, 32), :]
        squares = value * value
        return total + (squares[0:8] + squares[8:16]) + (squares[16:24] + squares[24:32])

    loads[0].wait()
    total = lax.fori_loop(0, 16, first_pass, jnp.zeros((8, NZ), F32), unroll=4)
    sums_begin(0, tile_of([total]))

    def second_pass(b, carry):
        x, y = lax.div(b, 4), pl.multiple_of(lax.rem(b, 4) * 32, 32)
        value = perm[x, pl.ds(y, 32), :].astype(F32)
        padp[x + 1, pl.ds(pl.multiple_of(y + 8, 8), 32), :] = value
        logp[x, pl.ds(y, 32), :] = jnp.log(value)
        zero = jnp.zeros((32, NZ), F32)
        prev[x, pl.ds(y, 32), :] = zero
        image[x, pl.ds(y, 32), :] = zero
        return carry

    for copy in loads[1:5]:
        copy.wait()
    lax.fori_loop(0, 16, second_pass, 0)
    mix_high, mix_low = split(mixv[:, 0:CH] * 0.5)
    rows_iota = lax.broadcasted_iota(jnp.int32, (128, 256), 0)
    lane_iota = lax.broadcasted_iota(jnp.int32, (128, 256), 1)
    same = lax.rem(rows_iota, 8) == lax.rem(lane_iota, 8)
    for n, piece in enumerate((mix_high, mix_low)):
        wide = dot(left_map[...], dot(piece, right_map[...]).astype(BF16))
        maps[n * 128 : (n + 1) * 128, :] = jnp.where(same, wide, 0.0).astype(BF16)

    lanes = lax.broadcasted_iota(jnp.int32, (32, NZ), 1)

    def around(ref, x, y, edge):
        own = ref[x + 1, pl.ds(y, 48), :]
        here = own[8:40]
        before = pltpu.roll(here, 1, 1)
        after = pltpu.roll(here, NZ - 1, 1)
        if edge:
            before = jnp.where(lanes == 0, here, before)
            after = jnp.where(lanes == NZ - 1, here, after)
        else:
            before = jnp.where(lanes == 0, 0.0, before)
            after = jnp.where(lanes == NZ - 1, 0.0, after)
        return here, (
            ref[x, pl.ds(pl.multiple_of(y + 8, 8), 32), :], ref[x + 2, pl.ds(pl.multiple_of(y + 8, 8), 32), :], own[7:39], own[9:41], before, after
        )

    def build_faces():
        for copy in perm_copies:
            copy.wait()
        padp[0, pl.ds(8, LY), :] = plx[...].astype(F32)
        padp[LX + 1, pl.ds(8, LY), :] = phx[...].astype(F32)
        for x in range(LX):
            padp[x + 1, pl.ds(0, 8), :] = ply[x].astype(F32)[8:16]
            padp[x + 1, pl.ds(LY + 8, 8), :] = phy[x].astype(F32)[0:8]

        @pl.when(row == 0)
        def _():
            padp[0, pl.ds(8, LY), :] = padp[1, pl.ds(8, LY), :]

        @pl.when(row == NR - 1)
        def _():
            padp[LX + 1, pl.ds(8, LY), :] = padp[LX, pl.ds(8, LY), :]

        @pl.when(col == 0)
        def _():
            for x in range(LX):
                padp[x + 1, pl.ds(0, 8), :] = jnp.broadcast_to(padp[x + 1, pl.ds(8, 8), :][0:1], (8, NZ))

        @pl.when(col == NC - 1)
        def _():
            for x in range(LX):
                padp[x + 1, pl.ds(LY + 8, 8), :] = jnp.broadcast_to(padp[x + 1, pl.ds(LY, 8), :][7:8], (8, NZ))

        def face_pass(b, carry):
            x, y = lax.div(b, 4), pl.multiple_of(lax.rem(b, 4) * 32, 32)
            here, others = around(padp, x, y, True)
            for n, other in enumerate(others):
                faces[n, x, pl.ds(y, 32), :] = 2.0 * here * other / (here + other)
            return carry

        lax.fori_loop(0, 16, face_pass, 0)

    for copy in loads[5:]:
        copy.wait()
    state[0] = jnp.broadcast_to(sums_end(0)[:, 0:1], (8, 128))
    state[1] = jnp.ones((8, 128), F32)

    mask_rows = lax.broadcasted_iota(jnp.int32, (16, 128), 0)
    mask_lanes = lax.broadcasted_iota(jnp.int32, (16, 128), 1)
    quad_mask = lax.rem(mask_rows, 4) == mask_lanes // 32
    low_half = lax.broadcasted_iota(jnp.int32, (8, 128), 0) < 4

    def iteration(i, carry):
        mean = state[0][0:1, 0:1] * (1.0 / CELLS) + 1e-6
        scale = jnp.sqrt(mean)
        inverse = 1.0 / scale

        def along_x(cq):
            whole = send(
                sf.at[cq, pl.ds(0, NR - 1)], vf.at[cq, pl.ds(0, NR - 1)], f_s.at[cq], f_r.at[cq], row, col
            )
            whole.wait_recv()
            whole.wait_send()
            high, low = split(vf[cq].reshape(256, 128))
            both = dot(xt[...], high)
            sx[cq] = (both[:64] + both[64:] + dot(xt[0:64, :], low)).reshape(NC, 8, 128)
            vx[cq, col] = sx[cq, col]

            def scatter(k, carry):
                to = lax.rem(col + k, NC)
                send(sx.at[cq, to], vx.at[cq, col], x_s.at[cq], x_r.at[cq], row, to).start()
                return carry

            lax.fori_loop(1, NC, scatter, 0, unroll=True)

        def forward(cq, carry):
            factors = [
                [jnp.full((8, NZ), lw[k, cq * 4 + c4] * 0.5, F32) for k in range(3)] for c4 in range(4)
            ]

            def lift_pass(b, carry):
                x, y = lax.div(b, 16), pl.multiple_of(lax.rem(b, 16) * 8, 8)
                scaled = res[x, pl.ds(y, 8), :] * inverse
                logs = logp[x, pl.ds(y, 8), :]
                for c4 in range(4):
                    c = cq * 4 + c4
                    half = factors[c4][0] * scaled + factors[c4][1] * logs + factors[c4][2]
                    inner = half * (2.0 * GELU_A + (8.0 * 0.044715 * GELU_A) * (half * half))
                    value = half + half * jnp.tanh(inner)
                    rest = value - value.astype(BF16).astype(F32)
                    lift[b, c] = jnp.concatenate([value, rest], axis=0).astype(BF16)
                return carry

            lax.fori_loop(0, 64, lift_pass, 0, unroll=16)
            tops, bottoms = [], []
            for c4 in range(4):
                c = cq * 4 + c4
                block = jnp.concatenate(
                    [lift[x * 16 : x * 16 + 16, c].reshape(256, NZ) for x in range(LX)], axis=1
                )
                deep = dot(block, tz[...]).reshape(16, 2, 8, 256)
                deep = (deep[:, 0] + deep[:, 1]).reshape(128, 256)
                tops.append(deep[:, :128])
                bottoms.append(deep[:, 128:])
            high, low = split(
                jnp.concatenate([jnp.concatenate(tops, axis=1), jnp.concatenate(bottoms, axis=1)], axis=0)
            )
            both = dot(yt[...], high)
            flat = both[:64] + both[64:] + dot(yt[0:64, :], low)
            turned = []
            for ri in range(2):
                square = jnp.concatenate(
                    [flat[ri * 32 : ri * 32 + 32, c4 * 128 : c4 * 128 + 128] for c4 in range(4)], axis=0
                )
                turned.append(square.T.reshape(NR, 8, 128))
            sf[cq] = jnp.concatenate(turned, axis=1)
            vf[cq, row] = sf[cq, row]

            def step(k, carry):
                to = lax.rem(row + k, NR)
                send(sf.at[cq, to], vf.at[cq, row], f_s.at[cq], f_r.at[cq], to, col).start()
                return carry

            lax.fori_loop(1, NR, step, 0, unroll=True)

            return carry

        lax.fori_loop(0, 4, forward, 0)
        def point_pass(b, carry):
            x, y = lax.div(b, 16), lax.rem(b, 16)
            both = dot(maps[...], lift[b].reshape(256, NZ))
            point[x, y] = (both[:128] + both[128:]).reshape(CH, 8, NZ)
            return carry

        along_x(0)
        along_x(1)
        lax.fori_loop(0, 40, point_pass, 0, unroll=8)
        along_x(2)
        along_x(3)
        lax.fori_loop(40, 64, point_pass, 0, unroll=8)

        @pl.when(i == 0)
        def _():
            build_faces()


        spectrum = []
        for cq in range(4):
            whole = send(
                sx.at[cq, pl.ds(0, NC - 1)], vx.at[cq, pl.ds(0, NC - 1)], x_s.at[cq], x_r.at[cq], row, col
            )
            whole.wait_recv()
            whole.wait_send()
            spectrum.append(jnp.sum(vx[cq], axis=0))

        stacks = []
        for ri in range(2):
            tiles = []
            for r in range(4):
                line = r * 2 + ri
                wide = [
                    jnp.broadcast_to(spectrum[q][line : line + 1], (8, 128)) for q in range(4)
                ]
                tall = jnp.concatenate(
                    [jnp.where(low_half, wide[0], wide[1]), jnp.where(low_half, wide[2], wide[3])], axis=0
                )
                tiles.append(jnp.where(quad_mask, tall, 0.0))
            stacks.append(jnp.concatenate(tiles, axis=1))
        high, low = split(jnp.concatenate(stacks, axis=0))
        both = dot(jnp.concatenate([high, low], axis=0), fold[...])
        ordered = both[:32] + both[32:]

        reals, imags = [], []
        for kz in range(2):
            real = jnp.zeros((CH, 64), F32)
            imag = jnp.zeros((CH, 64), F32)
            for c in range(CH):
                value_real = ordered[c : c + 1, kz * 64 : kz * 64 + 64]
                value_imag = ordered[CH + c : CH + c + 1, kz * 64 : kz * 64 + 64]
                weight_real = weight[0, kz, c]
                weight_imag = weight[1, kz, c]
                real = real + (weight_real * value_real - weight_imag * value_imag)
                imag = imag + (weight_real * value_imag + weight_imag * value_real)
            reals.append(real)
            imags.append(imag)
        mixed = jnp.concatenate([jnp.concatenate(reals, axis=1), jnp.concatenate(imags, axis=1)], axis=0)

        high, low = split(mixed)
        both = dot(jnp.concatenate([high, low], axis=0), spread[...])
        wide = both[:32] + both[32:]
        mask = jnp.concatenate([quad_mask, quad_mask], axis=0)
        tall = jnp.concatenate(
            [jnp.where(mask, wide[:, r * 128 : r * 128 + 128], 0.0) for r in range(4)], axis=0
        )
        high, low = split(tall)
        both = dot(gather[...], jnp.concatenate([high, low], axis=1))
        sm[...] = (both[:, :128] + both[:, 128:]).reshape(4, 8, 128)
        vm[col] = sm[...]

        def spread_out(k, carry):
            send(sm, vm.at[col], m_s, m_r, row, lax.rem(col + k, NC)).start()
            return carry

        lax.fori_loop(1, NC, spread_out, 0, unroll=True)
        whole = send(vm.at[pl.ds(0, NC - 1)], vm.at[pl.ds(0, NC - 1)], m_s, m_r, row, col)
        whole.wait_recv()
        whole.wait_send()

        high, low = split(jnp.concatenate([vm[:, oq].reshape(64, 128) for oq in range(4)], axis=1))
        back = dot(xi[...], jnp.concatenate([high, low, high], axis=0))
        for oq in range(4):
            sh[oq] = back[:, oq * 128 : oq * 128 + 128].reshape(NR, 16, 128)
            vh[oq, row] = sh[oq, row]

            def step(k, carry, oq=oq):
                to = lax.rem(row + k, NR)
                send(sh.at[oq, to], vh.at[oq, row], h_s.at[oq], h_r.at[oq], to, col).start()
                return carry

            lax.fori_loop(1, NR, step, 0, unroll=True)

        def clear(b, carry):
            x, y = lax.div(b, 4), pl.multiple_of(lax.rem(b, 4) * 32, 32)
            padk[x + 1, pl.ds(pl.multiple_of(y + 8, 8), 32), :] = jnp.full((32, NZ), pw[CH], F32)
            return carry

        lax.fori_loop(0, 16, clear, 0)

        def turn(oq):
            whole = send(
                sh.at[oq, pl.ds(0, NR - 1)], vh.at[oq, pl.ds(0, NR - 1)], h_s.at[oq], h_r.at[oq], row, col
            )
            whole.wait_recv()
            whole.wait_send()
            turned = [vh[oq, :, pl.ds(ri * 8, 8), :].reshape(128, 128).T for ri in range(2)]
            block = jnp.concatenate(
                [
                    jnp.concatenate([turned[ri][o4 * 32 : o4 * 32 + 32] for ri in range(2)], axis=0)
                    for o4 in range(4)
                ],
                axis=1,
            )
            high, low = split(block)
            back = dot(yi[...], jnp.concatenate([high, low, high], axis=0))
            for o4 in range(4):
                part = back[:, o4 * 128 : o4 * 128 + 128]
                high, low = split(jnp.concatenate([part[:128], part[128:]], axis=1))
                modes[o4] = jnp.concatenate([high, low, high], axis=1)

        def channels(oq, xs):
            for x in xs:
                for o4 in range(4):
                    o = oq * 4 + o4
                    bias = mw[o, CH] * 0.5
                    wave = dot(modes[o4], ti[x])
                    half = wave + point[x, :, o].reshape(LY, NZ) + bias
                    inner = half * (2.0 * GELU_A + (8.0 * 0.044715 * GELU_A) * (half * half))
                    hidden = pw[o] * (half + half * jnp.tanh(inner))
                    padk[x + 1, pl.ds(8, LY), :] += hidden

        def backward(oq, carry):
            turn(oq)
            channels(oq, range(LX))
            return carry

        def planes(xs):
            channels(3, xs)
            for x in xs:
                padk[x + 1, pl.ds(8, LY), :] = scale * padk[x + 1, pl.ds(8, LY), :]

        lax.fori_loop(0, 3, backward, 0)
        turn(3)
        planes((0, LX - 1))
        copies = [
            send(padk.at[LX, pl.ds(8, LY)], padk.at[0, pl.ds(8, LY)], halo_s.at[0], halo_r.at[0], up_row, col),
            send(padk.at[1, pl.ds(8, LY)], padk.at[LX + 1, pl.ds(8, LY)], halo_s.at[1], halo_r.at[1], down_row, col),
            send(
                padk.at[pl.ds(1, LX), pl.ds(LY, 8)], padk.at[pl.ds(1, LX), pl.ds(0, 8)],
                halo_s.at[2], halo_r.at[2], row, up_col,
            ),
            send(
                padk.at[pl.ds(1, LX), pl.ds(8, 8)], padk.at[pl.ds(1, LX), pl.ds(LY + 8, 8)],
                halo_s.at[3], halo_r.at[3], row, down_col,
            ),
        ]
        for copy in copies[:2]:
            copy.start()
        planes(range(1, LX - 1))
        for copy in copies[2:]:
            copy.start()
        keep = pltpu.make_async_copy(padk.at[pl.ds(1, LX), pl.ds(8, LY)], kept_out.at[i], kept_s)
        keep.start()
        for copy in copies:
            copy.wait()

        @pl.when(row == 0)
        def _():
            padk[0, pl.ds(8, LY), :] = jnp.zeros((LY, NZ), F32)

        @pl.when(row == NR - 1)
        def _():
            padk[LX + 1, pl.ds(8, LY), :] = jnp.zeros((LY, NZ), F32)

        @pl.when(col == 0)
        def _():
            padk[pl.ds(1, LX), pl.ds(0, 8), :] = jnp.zeros((LX, 8, NZ), F32)

        @pl.when(col == NC - 1)
        def _():
            padk[pl.ds(1, LX), pl.ds(LY + 8, 8), :] = jnp.zeros((LX, 8, NZ), F32)

        def fold8(value):
            return (value[0:8] + value[8:16]) + (value[16:24] + value[24:32])

        def operator_pass(b, totals):
            x, y = lax.div(b, 4), pl.multiple_of(lax.rem(b, 4) * 32, 32)
            here, others = around(padk, x, y, False)
            applied = jnp.zeros((32, NZ), F32)
            for n, other in enumerate(others):
                applied = applied + faces[n, x, pl.ds(y, 32), :] * (here - other)
            fresh[x, pl.ds(y, 32), :] = applied
            old_image = image[x, pl.ds(y, 32), :]
            residual = res[x, pl.ds(y, 32), :]
            old = prev[x, pl.ds(y, 32), :]
            terms = (
                here * applied, here * old_image, residual * here, residual * old, residual * applied,
                applied * applied,
            )
            return tuple(total + fold8(term) for total, term in zip(totals, terms))

        totals = lax.fori_loop(0, 16, operator_pass, tuple(jnp.zeros((8, NZ), F32) for _ in range(6)), unroll=2)
        sums_begin(1 + i, tile_of(totals))
        show = pltpu.make_async_copy(fresh, image_out.at[i], image_s)
        show.start()
        sums = sums_end(1 + i)
        k_ak, k_img, r_k, r_d, r_ak, ak_ak = [sums[:, n : n + 1] for n in range(6)]
        old_curve = state[1][0:1, 0:1]
        beta = k_img / old_curve
        curve = k_ak - 2.0 * beta * k_img + beta * beta * old_curve
        alpha = (r_k - beta * r_d) / curve

        @pl.when(i == 0)
        def _():
            def update(b, carry):
                x, y = lax.div(b, 4), pl.multiple_of(lax.rem(b, 4) * 32, 32)
                at = (x, pl.ds(y, 32), slice(None))
                applied = fresh[at]
                prev[at] = padk[x + 1, pl.ds(pl.multiple_of(y + 8, 8), 32), :]
                image[at] = applied
                res[at] = res[at] - alpha * applied
                return carry

            lax.fori_loop(0, 16, update, 0, unroll=4)

        steps_out[i] = jnp.broadcast_to(alpha, (8, 128))
        steps_out[2 + i] = jnp.broadcast_to(beta, (8, 128))
        keep.wait()
        show.wait()
        squares = state[0][0:1, 0:1] - 2.0 * alpha * r_ak + alpha * alpha * ak_ak
        state[0] = jnp.broadcast_to(jnp.maximum(squares, 0.0), (8, 128))
        state[1] = jnp.broadcast_to(curve, (8, 128))
        return carry

    lax.fori_loop(0, 2, iteration, 0)


def last(steps, rs, kept_in, image_in, sol_out, res_out, kept_out):
    first, second = steps[0, 0:1, 0:1], steps[1, 0:1, 0:1]
    first = first - second * steps[3, 0:1, 0:1]
    sol_out[...] = first * kept_in[0] + second * kept_in[1]
    res_out[...] = rs[...] - (first * image_in[0] + second * image_in[1])
    kept_out[...] = kept_in[...]


def local(right_side, permeability, lift_weight, spectral_weight, mix_weight, proj_weight):
    smem = pl.BlockSpec(memory_space=pltpu.SMEM)
    hbm = pl.BlockSpec(memory_space=pl.ANY)
    field = (LX, LY, NZ)
    dma = pltpu.SemaphoreType.DMA
    scratch = [
        pltpu.VMEM(field, F32),
        pltpu.VMEM(field, BF16),
        pltpu.VMEM((CH, CH + 1), F32),
        pltpu.VMEM((2, 2, CH, CH, 64), F32),
        pltpu.VMEM((LX * NZ, 256), BF16),
        pltpu.VMEM((LX, 768, NZ), BF16),
        pltpu.VMEM((128, 256), BF16),
        pltpu.VMEM((256, 192), BF16),
        pltpu.VMEM((512, 128), BF16),
        pltpu.VMEM((128, 512), BF16),
        pltpu.VMEM((32, 128), BF16),
        pltpu.VMEM((128, 16), BF16),
        pltpu.VMEM((16, 256), BF16),
        pltpu.VMEM((64, CH, 16, NZ), BF16),
        pltpu.VMEM((LX, 16, CH, 8, NZ), F32),
        pltpu.VMEM(field, F32),
        pltpu.VMEM((LX + 2, LY + 16, NZ), F32),
        pltpu.VMEM((LX + 2, LY + 16, NZ), F32),
        pltpu.VMEM((6,) + field, F32),
        pltpu.VMEM(field, F32),
        pltpu.VMEM(field, F32),
        pltpu.VMEM(field, F32),
        pltpu.VMEM((256, 256), BF16),
        pltpu.VMEM((128, 256), BF16),
        pltpu.VMEM((256, 192), BF16),
        pltpu.VMEM((LY, NZ), BF16),
        pltpu.VMEM((LY, NZ), BF16),
        pltpu.VMEM((LX, 16, NZ), BF16),
        pltpu.VMEM((LX, 16, NZ), BF16),
        pltpu.VMEM((4, NR, 16, 128), F32),
        pltpu.VMEM((4, NR, 16, 128), F32),
        pltpu.VMEM((4, NC, 8, 128), F32),
        pltpu.VMEM((4, NC, 8, 128), F32),
        pltpu.VMEM((4, 8, 128), F32),
        pltpu.VMEM((NC, 4, 8, 128), F32),
        pltpu.VMEM((4, NR, 16, 128), F32),
        pltpu.VMEM((4, NR, 16, 128), F32),
        pltpu.VMEM((4, LY, 768), BF16),
        pltpu.VMEM((3, 1, 128), F32),
        pltpu.VMEM((3, NR * NC, 1, 128), F32),
        pltpu.VMEM((2, 8, 128), F32),
        dma((4,)), dma((4,)), dma((4,)), dma((4,)), dma((4,)), dma((4,)),
        dma((4,)), dma((4,)), dma, dma, dma((4,)), dma((4,)),
        dma((3,)), dma((3,)), dma((15,)), dma, dma,
    ]
    constants = [jnp.asarray(t) for t in tables()]
    pair = jax.ShapeDtypeStruct((2,) + field, F32)
    kept, images, steps = pl.pallas_call(
        kernel,
        out_shape=[pair, pair, jax.ShapeDtypeStruct((4, 8, 128), F32)],
        in_specs=[hbm, hbm, smem, smem, smem] + [hbm] * 13,
        out_specs=[hbm, hbm, pl.BlockSpec(memory_space=pltpu.VMEM)],
        scratch_shapes=scratch,
        compiler_params=pltpu.CompilerParams(
            collective_id=0, has_side_effects=True, vmem_limit_bytes=56 * 1024 * 1024
        ),
    )(
        right_side, permeability, lift_weight.T, mix_weight, proj_weight, mix_weight,
        spectral_weight, *constants,
    )
    plane = (2, LY, NZ)
    one = pl.BlockSpec(plane, lambda x: (x, 0, 0))
    two = pl.BlockSpec((2,) + plane, lambda x: (0, x, 0, 0))
    return pl.pallas_call(
        last,
        grid=(LX // 2,),
        out_shape=[jax.ShapeDtypeStruct(field, F32), jax.ShapeDtypeStruct(field, F32), pair],
        in_specs=[pl.BlockSpec((4, 8, 128), lambda x: (0, 0, 0)), one, two, two],
        out_specs=[one, one, two],
    )(steps, right_side, kept, images)


def solution(mesh):
    placed = (
        P("row", "col", None), P("row", "col", None), P(), P(None, "row", None, None, "col"), P(), P(),
    )
    return jax.shard_map(
        local,
        mesh=mesh,
        in_specs=placed,
        out_specs=(P("row", "col", None), P("row", "col", None), P(None, "row", "col", None)),
        check_vma=False,
    )
```

```python
import jax
import jax.numpy as jnp
import ml_dtypes
import numpy as np
from jax import lax
from jax.experimental import pallas as pl
from jax.experimental.pallas import tpu as pltpu
from jax.sharding import PartitionSpec as P

F32 = jnp.float32
BF16 = jnp.bfloat16
MESH = pl.DeviceIdType.MESH
NR, NC = 16, 8
NX, NY, NZ = 64, 1024, 256
LX, LY = NX // NR, NY // NC
CH = 16
CELLS = float(NX * NY * NZ)
GELU_A = float(np.sqrt(2.0 / np.pi))


def pieces(table):
    high = table.astype(ml_dtypes.bfloat16)
    low = (table - high.astype(np.float64)).astype(ml_dtypes.bfloat16)
    return high, low


def waves(freqs, places, length):
    angle = 2.0 * np.pi * ((freqs[None, :] * places[:, None]) % length) / length
    return np.cos(angle), np.sin(angle)


def tables():
    cz, sz = waves(np.arange(32), np.arange(NZ), NZ)
    tz = np.zeros((LX, NZ, 2, 32, LX))
    ti = np.zeros((2, 32, LX, LX, NZ))
    for x in range(LX):
        tz[x, :, 0, :, x] = cz
        tz[x, :, 1, :, x] = sz
        ti[0, :, x, x, :] = cz.T
        ti[1, :, x, x, :] = -sz.T
    tz = pieces(tz.reshape(LX * NZ, 256))[0]
    ti_high, ti_low = pieces(ti.reshape(256, LX * NZ))
    ti = np.concatenate([ti_high, ti_high, ti_low], axis=0)
    ti = np.ascontiguousarray(ti.reshape(768, LX, NZ).transpose(1, 0, 2))

    yt = np.zeros((NC, 2, 32, 2, LY))
    yi = np.zeros((NC, 2, LY, 2, 32))
    for col in range(NC):
        cy, sy = waves(np.arange(-16, 16), np.arange(LY) + col * LY, NY)
        yt[col, 0, :, 0] = cy.T
        yt[col, 0, :, 1] = -sy.T
        yt[col, 1, :, 0] = -sy.T
        yt[col, 1, :, 1] = -cy.T
        yi[col, 0, :, 0] = cy
        yi[col, 0, :, 1] = -sy
        yi[col, 1, :, 0] = sy
        yi[col, 1, :, 1] = cy
    yt = np.concatenate(pieces(yt.reshape(NC, 64, 256)), axis=1)
    yi_high, yi_low = pieces(yi.reshape(NC, 256, 64))
    yi = np.concatenate([yi_high, yi_high, yi_low], axis=2)

    cx, sx = waves(np.arange(-8, 8), np.arange(NX), NX)
    cx = cx.reshape(NR, LX, NC, 2)
    sx = sx.reshape(NR, LX, NC, 2)
    xt = np.zeros((NC, 2, 2, 2, NR, 2, 2, LX))
    xi = np.zeros((NR, 2, 2, LX, NC, 2, 2, 2))
    for kz in range(2):
        forward_cos = cx.transpose(2, 3, 0, 1)
        forward_sin = sx.transpose(2, 3, 0, 1)
        xt[:, kz, :, 0, :, 0, kz, :] = forward_cos
        xt[:, kz, :, 0, :, 1, kz, :] = forward_sin
        xt[:, kz, :, 1, :, 1, kz, :] = forward_cos
        xt[:, kz, :, 1, :, 0, kz, :] = -forward_sin
        xi[:, 0, kz, :, :, kz, :, 0] = cx
        xi[:, 0, kz, :, :, kz, :, 1] = -sx
        xi[:, 1, kz, :, :, kz, :, 1] = cx
        xi[:, 1, kz, :, :, kz, :, 0] = sx
    xt = np.concatenate(pieces(xt.reshape(64, 256)), axis=0)
    xi_high, xi_low = pieces(xi.reshape(256, 64) * (0.5 / CELLS))
    xi = np.concatenate([xi_high, xi_high, xi_low], axis=1)

    fold = np.zeros((4, 4, 32, 4, 32))
    for r in range(4):
        for c in range(4):
            fold[r, c, :, r, :] = np.eye(32)
    fold = fold.reshape(512, 128)
    spread = np.ascontiguousarray(fold.T)
    gather = np.zeros((4, 4, 2, 4, 2, 16))
    for quad in range(4):
        for r in range(4):
            for ri in range(2):
                gather[quad, r, ri, r, ri, quad * 4 : quad * 4 + 4] = 1.0
    gather = gather.reshape(32, 128)
    left = np.kron(np.eye(16), np.ones((8, 1)))
    right = np.zeros((16, 16, 2, 8))
    for c in range(16):
        right[c, c] = 1.0
    right = right.reshape(16, 256)
    b16 = lambda a: a.astype(ml_dtypes.bfloat16)
    return tz, ti, yt, yi, xt, xi, b16(fold), b16(spread), b16(gather), b16(left), b16(right)


def split(value):
    high = value.astype(BF16)
    return high, (value - high.astype(F32)).astype(BF16)


def dot(left, right):
    return jnp.dot(left, right, preferred_element_type=F32)


def kernel(
    rs, perm_in, lw, mw, pw, mix_in, weight_in,
    tz_in, ti_in, yt_all, yi_all, xt_in, xi_in, fold_in, spread_in, gather_in, left_in, right_in,
    kept_out, image_out, steps_out,
    res, perm, mixv, weight, tz, ti, xt, xi, fold, spread, gather, left_map, right_map,
    lift, point, logp, padk, padp, faces, prev, image, fresh, maps, yt, yi,
    plx, phx, ply, phy,
    sf, vf, sx, vx, sm, vm, sh, vh, modes,
    asrc, aall, state,
    perm_s, perm_r, halo_s, halo_r, f_s, f_r, x_s, x_r, m_s, m_r, h_s, h_r, ac_s, ac_r, table_s, kept_s, image_s,
):
    row = lax.axis_index("row")
    col = lax.axis_index("col")
    up_row, down_row = lax.rem(row + 1, NR), lax.rem(row + NR - 1, NR)
    up_col, down_col = lax.rem(col + 1, NC), lax.rem(col + NC - 1, NC)

    def send(src, dst, s, r, to_row, to_col):
        return pltpu.make_async_remote_copy(
            src_ref=src, dst_ref=dst, send_sem=s, recv_sem=r, device_id=(to_row, to_col), device_id_type=MESH
        )

    loads = [
        (rs, res), (perm_in, perm), (mix_in, mixv), (left_in, left_map), (right_in, right_map), (tz_in, tz),
        (yt_all.at[col], yt), (xt_in, xt), (weight_in, weight), (fold_in, fold), (spread_in, spread),
        (gather_in, gather), (xi_in, xi), (yi_all.at[col], yi), (ti_in, ti),
    ]
    loads = [pltpu.make_async_copy(src, dst, table_s.at[n]) for n, (src, dst) in enumerate(loads)]
    for copy in loads:
        copy.start()

    barrier = pltpu.get_barrier_semaphore()

    def to_all(act):
        for other in range(1, NC):
            act(row, lax.rem(col + other, NC))

        def step(k, carry):
            to_row = lax.rem(row + k, NR)
            for other in range(NC):
                act(to_row, lax.rem(col + other, NC))
            return carry

        lax.fori_loop(1, NR, step, 0)

    to_all(lambda r, c: pl.semaphore_signal(barrier, 1, device_id=(r, c), device_id_type=MESH))
    pl.semaphore_wait(barrier, NR * NC - 1)

    perm_copies = [
        send(perm_in.at[LX - 1], plx, perm_s.at[0], perm_r.at[0], up_row, col),
        send(perm_in.at[0], phx, perm_s.at[1], perm_r.at[1], down_row, col),
        send(perm_in.at[:, pl.ds(LY - 16, 16), :], ply, perm_s.at[2], perm_r.at[2], row, up_col),
        send(perm_in.at[:, pl.ds(0, 16), :], phy, perm_s.at[3], perm_r.at[3], row, down_col),
    ]
    for copy in perm_copies:
        copy.start()

    def sums_begin(u, line):
        me = row * NC + col
        asrc[u] = line
        aall[u, me] = line
        to_all(lambda r, c: send(asrc.at[u], aall.at[u, me], ac_s.at[u], ac_r.at[u], r, c).start())

    def sums_end(u):
        whole = send(
            aall.at[u, pl.ds(0, NR * NC - 1)], aall.at[u, pl.ds(0, NR * NC - 1)], ac_s.at[u], ac_r.at[u], row, col
        )
        whole.wait_recv()
        whole.wait_send()
        return jnp.sum(aall[u], axis=0)

    def tile_of(parts):
        rows = []
        for part in parts:
            line = jnp.sum(part, axis=0, keepdims=True)
            rows.append(line[:, :128] + line[:, 128:])
        index = lax.broadcasted_iota(jnp.int32, (8, 128), 0)
        tile = jnp.zeros((8, 128), F32)
        for i, line in enumerate(rows):
            tile = jnp.where(index == i, jnp.broadcast_to(line, (8, 128)), tile)
        each = jnp.broadcast_to(jnp.sum(tile, axis=1, keepdims=True), (8, 128))
        lane = lax.broadcasted_iota(jnp.int32, (8, 128), 1)
        return jnp.sum(jnp.where(index == lane, each, 0.0), axis=0, keepdims=True)

    def first_pass(b, total):
        x, y = lax.div(b, 4), pl.multiple_of(lax.rem(b, 4) * 32, 32)
        value = res[x, pl.ds(y, 32), :]
        squares = value * value
        return total + (squares[0:8] + squares[8:16]) + (squares[16:24] + squares[24:32])

    loads[0].wait()
    total = lax.fori_loop(0, 16, first_pass, jnp.zeros((8, NZ), F32), unroll=4)
    sums_begin(0, tile_of([total]))

    def second_pass(b, carry):
        x, y = lax.div(b, 4), pl.multiple_of(lax.rem(b, 4) * 32, 32)
        value = perm[x, pl.ds(y, 32), :].astype(F32)
        padp[x + 1, pl.ds(pl.multiple_of(y + 8, 8), 32), :] = value
        logp[x, pl.ds(y, 32), :] = jnp.log(value)
        zero = jnp.zeros((32, NZ), F32)
        prev[x, pl.ds(y, 32), :] = zero
        image[x, pl.ds(y, 32), :] = zero
        return carry

    for copy in loads[1:5]:
        copy.wait()
    lax.fori_loop(0, 16, second_pass, 0, unroll=2)
    mix_high, mix_low = split(mixv[:, 0:CH] * 0.5)
    rows_iota = lax.broadcasted_iota(jnp.int32, (128, 256), 0)
    lane_iota = lax.broadcasted_iota(jnp.int32, (128, 256), 1)
    same = lax.rem(rows_iota, 8) == lax.rem(lane_iota, 8)
    for n, piece in enumerate((mix_high, mix_low)):
        wide = dot(left_map[...], dot(piece, right_map[...]).astype(BF16))
        maps[n * 128 : (n + 1) * 128, :] = jnp.where(same, wide, 0.0).astype(BF16)

    lanes = lax.broadcasted_iota(jnp.int32, (32, NZ), 1)

    def around(ref, x, y, edge):
        own = ref[x + 1, pl.ds(y, 48), :]
        here = own[8:40]
        before = pltpu.roll(here, 1, 1)
        after = pltpu.roll(here, NZ - 1, 1)
        if edge:
            before = jnp.where(lanes == 0, here, before)
            after = jnp.where(lanes == NZ - 1, here, after)
        else:
            before = jnp.where(lanes == 0, 0.0, before)
            after = jnp.where(lanes == NZ - 1, 0.0, after)
        return here, (
            ref[x, pl.ds(pl.multiple_of(y + 8, 8), 32), :], ref[x + 2, pl.ds(pl.multiple_of(y + 8, 8), 32), :], own[7:39], own[9:41], before, after
        )

    def build_faces():
        for copy in perm_copies:
            copy.wait()
        padp[0, pl.ds(8, LY), :] = plx[...].astype(F32)
        padp[LX + 1, pl.ds(8, LY), :] = phx[...].astype(F32)
        for x in range(LX):
            padp[x + 1, pl.ds(0, 8), :] = ply[x].astype(F32)[8:16]
            padp[x + 1, pl.ds(LY + 8, 8), :] = phy[x].astype(F32)[0:8]

        @pl.when(row == 0)
        def _():
            padp[0, pl.ds(8, LY), :] = padp[1, pl.ds(8, LY), :]

        @pl.when(row == NR - 1)
        def _():
            padp[LX + 1, pl.ds(8, LY), :] = padp[LX, pl.ds(8, LY), :]

        @pl.when(col == 0)
        def _():
            for x in range(LX):
                padp[x + 1, pl.ds(0, 8), :] = jnp.broadcast_to(padp[x + 1, pl.ds(8, 8), :][0:1], (8, NZ))

        @pl.when(col == NC - 1)
        def _():
            for x in range(LX):
                padp[x + 1, pl.ds(LY + 8, 8), :] = jnp.broadcast_to(padp[x + 1, pl.ds(LY, 8), :][7:8], (8, NZ))

        def face_pass(b, carry):
            x, y = lax.div(b, 4), pl.multiple_of(lax.rem(b, 4) * 32, 32)
            here, others = around(padp, x, y, True)
            for n, other in enumerate(others):
                faces[n, x, pl.ds(y, 32), :] = 2.0 * here * other / (here + other)
            return carry

        lax.fori_loop(0, 16, face_pass, 0, unroll=2)

    for copy in loads[5:]:
        copy.wait()
    state[0] = jnp.broadcast_to(sums_end(0)[:, 0:1], (8, 128))
    state[1] = jnp.ones((8, 128), F32)

    mask_rows = lax.broadcasted_iota(jnp.int32, (16, 128), 0)
    mask_lanes = lax.broadcasted_iota(jnp.int32, (16, 128), 1)
    quad_mask = lax.rem(mask_rows, 4) == mask_lanes // 32
    low_half = lax.broadcasted_iota(jnp.int32, (8, 128), 0) < 4

    def iteration(i, carry):
        mean = state[0][0:1, 0:1] * (1.0 / CELLS) + 1e-6
        scale = jnp.sqrt(mean)
        inverse = 1.0 / scale

        def along_x(cq):
            whole = send(
                sf.at[cq, pl.ds(0, NR - 1)], vf.at[cq, pl.ds(0, NR - 1)], f_s.at[cq], f_r.at[cq], row, col
            )
            whole.wait_recv()
            whole.wait_send()
            high, low = split(vf[cq].reshape(256, 128))
            both = dot(xt[...], high)
            sx[cq] = (both[:64] + both[64:] + dot(xt[0:64, :], low)).reshape(NC, 8, 128)
            vx[cq, col] = sx[cq, col]

            def scatter(k, carry):
                to = lax.rem(col + k, NC)
                send(sx.at[cq, to], vx.at[cq, col], x_s.at[cq], x_r.at[cq], row, to).start()
                return carry

            lax.fori_loop(1, NC, scatter, 0, unroll=True)

        def forward(cq, carry):
            factors = [
                [jnp.full((8, NZ), lw[k, cq * 4 + c4] * 0.5, F32) for k in range(3)] for c4 in range(4)
            ]

            def lift_pass(b, carry):
                x, y = lax.div(b, 16), pl.multiple_of(lax.rem(b, 16) * 8, 8)
                scaled = res[x, pl.ds(y, 8), :] * inverse
                logs = logp[x, pl.ds(y, 8), :]
                for c4 in range(4):
                    c = cq * 4 + c4
                    half = factors[c4][0] * scaled + factors[c4][1] * logs + factors[c4][2]
                    inner = half * (2.0 * GELU_A + (8.0 * 0.044715 * GELU_A) * (half * half))
                    value = half + half * jnp.tanh(inner)
                    rest = value - value.astype(BF16).astype(F32)
                    lift[b, c] = jnp.concatenate([value, rest], axis=0).astype(BF16)
                return carry

            lax.fori_loop(0, 64, lift_pass, 0, unroll=16)
            tops, bottoms = [], []
            for c4 in range(4):
                c = cq * 4 + c4
                block = jnp.concatenate(
                    [lift[x * 16 : x * 16 + 16, c].reshape(256, NZ) for x in range(LX)], axis=1
                )
                deep = dot(block, tz[...]).reshape(16, 2, 8, 256)
                deep = (deep[:, 0] + deep[:, 1]).reshape(128, 256)
                tops.append(deep[:, :128])
                bottoms.append(deep[:, 128:])
            high, low = split(
                jnp.concatenate([jnp.concatenate(tops, axis=1), jnp.concatenate(bottoms, axis=1)], axis=0)
            )
            both = dot(yt[...], high)
            flat = both[:64] + both[64:] + dot(yt[0:64, :], low)
            turned = []
            for ri in range(2):
                square = jnp.concatenate(
                    [flat[ri * 32 : ri * 32 + 32, c4 * 128 : c4 * 128 + 128] for c4 in range(4)], axis=0
                )
                turned.append(square.T.reshape(NR, 8, 128))
            sf[cq] = jnp.concatenate(turned, axis=1)
            vf[cq, row] = sf[cq, row]

            def step(k, carry):
                to = lax.rem(row + k, NR)
                send(sf.at[cq, to], vf.at[cq, row], f_s.at[cq], f_r.at[cq], to, col).start()
                return carry

            lax.fori_loop(1, NR, step, 0, unroll=True)

            return carry

        lax.fori_loop(0, 4, forward, 0)
        def point_pass(b, carry):
            x, y = lax.div(b, 16), lax.rem(b, 16)
            both = dot(maps[...], lift[b].reshape(256, NZ))
            point[x, y] = (both[:128] + both[128:]).reshape(CH, 8, NZ)
            return carry

        along_x(0)
        along_x(1)
        lax.fori_loop(0, 40, point_pass, 0, unroll=8)
        along_x(2)
        along_x(3)
        lax.fori_loop(40, 64, point_pass, 0, unroll=8)

        @pl.when(i == 0)
        def _():
            build_faces()


        spectrum = []
        for cq in range(4):
            whole = send(
                sx.at[cq, pl.ds(0, NC - 1)], vx.at[cq, pl.ds(0, NC - 1)], x_s.at[cq], x_r.at[cq], row, col
            )
            whole.wait_recv()
            whole.wait_send()
            spectrum.append(jnp.sum(vx[cq], axis=0))

        stacks = []
        for ri in range(2):
            tiles = []
            for r in range(4):
                line = r * 2 + ri
                wide = [
                    jnp.broadcast_to(spectrum[q][line : line + 1], (8, 128)) for q in range(4)
                ]
                tall = jnp.concatenate(
                    [jnp.where(low_half, wide[0], wide[1]), jnp.where(low_half, wide[2], wide[3])], axis=0
                )
                tiles.append(jnp.where(quad_mask, tall, 0.0))
            stacks.append(jnp.concatenate(tiles, axis=1))
        high, low = split(jnp.concatenate(stacks, axis=0))
        both = dot(jnp.concatenate([high, low], axis=0), fold[...])
        ordered = both[:32] + both[32:]

        reals, imags = [], []
        for kz in range(2):
            real = jnp.zeros((CH, 64), F32)
            imag = jnp.zeros((CH, 64), F32)
            for c in range(CH):
                value_real = ordered[c : c + 1, kz * 64 : kz * 64 + 64]
                value_imag = ordered[CH + c : CH + c + 1, kz * 64 : kz * 64 + 64]
                weight_real = weight[0, kz, c]
                weight_imag = weight[1, kz, c]
                real = real + (weight_real * value_real - weight_imag * value_imag)
                imag = imag + (weight_real * value_imag + weight_imag * value_real)
            reals.append(real)
            imags.append(imag)
        mixed = jnp.concatenate([jnp.concatenate(reals, axis=1), jnp.concatenate(imags, axis=1)], axis=0)

        high, low = split(mixed)
        both = dot(jnp.concatenate([high, low], axis=0), spread[...])
        wide = both[:32] + both[32:]
        mask = jnp.concatenate([quad_mask, quad_mask], axis=0)
        tall = jnp.concatenate(
            [jnp.where(mask, wide[:, r * 128 : r * 128 + 128], 0.0) for r in range(4)], axis=0
        )
        high, low = split(tall)
        both = dot(gather[...], jnp.concatenate([high, low], axis=1))
        sm[...] = (both[:, :128] + both[:, 128:]).reshape(4, 8, 128)
        vm[col] = sm[...]

        def spread_out(k, carry):
            send(sm, vm.at[col], m_s, m_r, row, lax.rem(col + k, NC)).start()
            return carry

        lax.fori_loop(1, NC, spread_out, 0, unroll=True)
        whole = send(vm.at[pl.ds(0, NC - 1)], vm.at[pl.ds(0, NC - 1)], m_s, m_r, row, col)
        whole.wait_recv()
        whole.wait_send()

        high, low = split(jnp.concatenate([vm[:, oq].reshape(64, 128) for oq in range(4)], axis=1))
        back = dot(xi[...], jnp.concatenate([high, low, high], axis=0))
        for oq in range(4):
            sh[oq] = back[:, oq * 128 : oq * 128 + 128].reshape(NR, 16, 128)
            vh[oq, row] = sh[oq, row]

            def step(k, carry, oq=oq):
                to = lax.rem(row + k, NR)
                send(sh.at[oq, to], vh.at[oq, row], h_s.at[oq], h_r.at[oq], to, col).start()
                return carry

            lax.fori_loop(1, NR, step, 0, unroll=True)

        def clear(b, carry):
            x, y = lax.div(b, 4), pl.multiple_of(lax.rem(b, 4) * 32, 32)
            padk[x + 1, pl.ds(pl.multiple_of(y + 8, 8), 32), :] = jnp.full((32, NZ), pw[CH], F32)
            return carry

        lax.fori_loop(0, 16, clear, 0, unroll=4)

        def turn(oq):
            whole = send(
                sh.at[oq, pl.ds(0, NR - 1)], vh.at[oq, pl.ds(0, NR - 1)], h_s.at[oq], h_r.at[oq], row, col
            )
            whole.wait_recv()
            whole.wait_send()
            turned = [vh[oq, :, pl.ds(ri * 8, 8), :].reshape(128, 128).T for ri in range(2)]
            block = jnp.concatenate(
                [
                    jnp.concatenate([turned[ri][o4 * 32 : o4 * 32 + 32] for ri in range(2)], axis=0)
                    for o4 in range(4)
                ],
                axis=1,
            )
            high, low = split(block)
            back = dot(yi[...], jnp.concatenate([high, low, high], axis=0))
            for o4 in range(4):
                part = back[:, o4 * 128 : o4 * 128 + 128]
                high, low = split(jnp.concatenate([part[:128], part[128:]], axis=1))
                modes[o4] = jnp.concatenate([high, low, high], axis=1)

        def channels(oq, xs):
            for x in xs:
                for o4 in range(4):
                    o = oq * 4 + o4
                    bias = mw[o, CH] * 0.5
                    wave = dot(modes[o4], ti[x])
                    half = wave + point[x, :, o].reshape(LY, NZ) + bias
                    inner = half * (2.0 * GELU_A + (8.0 * 0.044715 * GELU_A) * (half * half))
                    hidden = pw[o] * (half + half * jnp.tanh(inner))
                    padk[x + 1, pl.ds(8, LY), :] += hidden

        def backward(oq, carry):
            turn(oq)
            channels(oq, range(LX))
            return carry

        def planes(xs):
            channels(3, xs)
            for x in xs:
                padk[x + 1, pl.ds(8, LY), :] = scale * padk[x + 1, pl.ds(8, LY), :]

        lax.fori_loop(0, 3, backward, 0)
        turn(3)
        planes((0, LX - 1))
        copies = [
            send(padk.at[LX, pl.ds(8, LY)], padk.at[0, pl.ds(8, LY)], halo_s.at[0], halo_r.at[0], up_row, col),
            send(padk.at[1, pl.ds(8, LY)], padk.at[LX + 1, pl.ds(8, LY)], halo_s.at[1], halo_r.at[1], down_row, col),
            send(
                padk.at[pl.ds(1, LX), pl.ds(LY, 8)], padk.at[pl.ds(1, LX), pl.ds(0, 8)],
                halo_s.at[2], halo_r.at[2], row, up_col,
            ),
            send(
                padk.at[pl.ds(1, LX), pl.ds(8, 8)], padk.at[pl.ds(1, LX), pl.ds(LY + 8, 8)],
                halo_s.at[3], halo_r.at[3], row, down_col,
            ),
        ]
        for copy in copies[:2]:
            copy.start()
        planes(range(1, LX - 1))
        for copy in copies[2:]:
            copy.start()
        keep = pltpu.make_async_copy(padk.at[pl.ds(1, LX), pl.ds(8, LY)], kept_out.at[i], kept_s)
        keep.start()
        for copy in copies:
            copy.wait()

        @pl.when(row == 0)
        def _():
            padk[0, pl.ds(8, LY), :] = jnp.zeros((LY, NZ), F32)

        @pl.when(row == NR - 1)
        def _():
            padk[LX + 1, pl.ds(8, LY), :] = jnp.zeros((LY, NZ), F32)

        @pl.when(col == 0)
        def _():
            padk[pl.ds(1, LX), pl.ds(0, 8), :] = jnp.zeros((LX, 8, NZ), F32)

        @pl.when(col == NC - 1)
        def _():
            padk[pl.ds(1, LX), pl.ds(LY + 8, 8), :] = jnp.zeros((LX, 8, NZ), F32)

        def fold8(value):
            return (value[0:8] + value[8:16]) + (value[16:24] + value[24:32])

        def operator_pass(b, totals):
            x, y = lax.div(b, 4), pl.multiple_of(lax.rem(b, 4) * 32, 32)
            here, others = around(padk, x, y, False)
            applied = jnp.zeros((32, NZ), F32)
            for n, other in enumerate(others):
                applied = applied + faces[n, x, pl.ds(y, 32), :] * (here - other)
            fresh[x, pl.ds(y, 32), :] = applied
            old_image = image[x, pl.ds(y, 32), :]
            residual = res[x, pl.ds(y, 32), :]
            old = prev[x, pl.ds(y, 32), :]
            terms = (
                here * applied, here * old_image, residual * here, residual * old, residual * applied,
                applied * applied,
            )
            return tuple(total + fold8(term) for total, term in zip(totals, terms))

        totals = lax.fori_loop(0, 16, operator_pass, tuple(jnp.zeros((8, NZ), F32) for _ in range(6)), unroll=4)
        sums_begin(1 + i, tile_of(totals))
        show = pltpu.make_async_copy(fresh, image_out.at[i], image_s)
        show.start()
        sums = sums_end(1 + i)
        k_ak, k_img, r_k, r_d, r_ak, ak_ak = [sums[:, n : n + 1] for n in range(6)]
        old_curve = state[1][0:1, 0:1]
        beta = k_img / old_curve
        curve = k_ak - 2.0 * beta * k_img + beta * beta * old_curve
        alpha = (r_k - beta * r_d) / curve

        @pl.when(i == 0)
        def _():
            def update(b, carry):
                x, y = lax.div(b, 4), pl.multiple_of(lax.rem(b, 4) * 32, 32)
                at = (x, pl.ds(y, 32), slice(None))
                applied = fresh[at]
                prev[at] = padk[x + 1, pl.ds(pl.multiple_of(y + 8, 8), 32), :]
                image[at] = applied
                res[at] = res[at] - alpha * applied
                return carry

            lax.fori_loop(0, 16, update, 0, unroll=4)

        steps_out[i] = jnp.broadcast_to(alpha, (8, 128))
        steps_out[2 + i] = jnp.broadcast_to(beta, (8, 128))
        keep.wait()
        show.wait()
        squares = state[0][0:1, 0:1] - 2.0 * alpha * r_ak + alpha * alpha * ak_ak
        state[0] = jnp.broadcast_to(jnp.maximum(squares, 0.0), (8, 128))
        state[1] = jnp.broadcast_to(curve, (8, 128))
        return carry

    lax.fori_loop(0, 2, iteration, 0)


def last(steps, rs, kept_in, image_in, sol_out, res_out, kept_out):
    first, second = steps[0, 0:1, 0:1], steps[1, 0:1, 0:1]
    first = first - second * steps[3, 0:1, 0:1]
    sol_out[...] = first * kept_in[0] + second * kept_in[1]
    res_out[...] = rs[...] - (first * image_in[0] + second * image_in[1])
    kept_out[...] = kept_in[...]


def local(right_side, permeability, lift_weight, spectral_weight, mix_weight, proj_weight):
    smem = pl.BlockSpec(memory_space=pltpu.SMEM)
    hbm = pl.BlockSpec(memory_space=pl.ANY)
    field = (LX, LY, NZ)
    dma = pltpu.SemaphoreType.DMA
    scratch = [
        pltpu.VMEM(field, F32),
        pltpu.VMEM(field, BF16),
        pltpu.VMEM((CH, CH + 1), F32),
        pltpu.VMEM((2, 2, CH, CH, 64), F32),
        pltpu.VMEM((LX * NZ, 256), BF16),
        pltpu.VMEM((LX, 768, NZ), BF16),
        pltpu.VMEM((128, 256), BF16),
        pltpu.VMEM((256, 192), BF16),
        pltpu.VMEM((512, 128), BF16),
        pltpu.VMEM((128, 512), BF16),
        pltpu.VMEM((32, 128), BF16),
        pltpu.VMEM((128, 16), BF16),
        pltpu.VMEM((16, 256), BF16),
        pltpu.VMEM((64, CH, 16, NZ), BF16),
        pltpu.VMEM((LX, 16, CH, 8, NZ), F32),
        pltpu.VMEM(field, F32),
        pltpu.VMEM((LX + 2, LY + 16, NZ), F32),
        pltpu.VMEM((LX + 2, LY + 16, NZ), F32),
        pltpu.VMEM((6,) + field, F32),
        pltpu.VMEM(field, F32),
        pltpu.VMEM(field, F32),
        pltpu.VMEM(field, F32),
        pltpu.VMEM((256, 256), BF16),
        pltpu.VMEM((128, 256), BF16),
        pltpu.VMEM((256, 192), BF16),
        pltpu.VMEM((LY, NZ), BF16),
        pltpu.VMEM((LY, NZ), BF16),
        pltpu.VMEM((LX, 16, NZ), BF16),
        pltpu.VMEM((LX, 16, NZ), BF16),
        pltpu.VMEM((4, NR, 16, 128), F32),
        pltpu.VMEM((4, NR, 16, 128), F32),
        pltpu.VMEM((4, NC, 8, 128), F32),
        pltpu.VMEM((4, NC, 8, 128), F32),
        pltpu.VMEM((4, 8, 128), F32),
        pltpu.VMEM((NC, 4, 8, 128), F32),
        pltpu.VMEM((4, NR, 16, 128), F32),
        pltpu.VMEM((4, NR, 16, 128), F32),
        pltpu.VMEM((4, LY, 768), BF16),
        pltpu.VMEM((3, 1, 128), F32),
        pltpu.VMEM((3, NR * NC, 1, 128), F32),
        pltpu.VMEM((2, 8, 128), F32),
        dma((4,)), dma((4,)), dma((4,)), dma((4,)), dma((4,)), dma((4,)),
        dma((4,)), dma((4,)), dma, dma, dma((4,)), dma((4,)),
        dma((3,)), dma((3,)), dma((15,)), dma, dma,
    ]
    constants = [jnp.asarray(t) for t in tables()]
    pair = jax.ShapeDtypeStruct((2,) + field, F32)
    kept, images, steps = pl.pallas_call(
        kernel,
        out_shape=[pair, pair, jax.ShapeDtypeStruct((4, 8, 128), F32)],
        in_specs=[hbm, hbm, smem, smem, smem] + [hbm] * 13,
        out_specs=[hbm, hbm, pl.BlockSpec(memory_space=pltpu.VMEM)],
        scratch_shapes=scratch,
        compiler_params=pltpu.CompilerParams(
            collective_id=0, has_side_effects=True, vmem_limit_bytes=56 * 1024 * 1024
        ),
    )(
        right_side, permeability, lift_weight.T, mix_weight, proj_weight, mix_weight,
        spectral_weight, *constants,
    )
    plane = (2, LY, NZ)
    one = pl.BlockSpec(plane, lambda x: (x, 0, 0))
    two = pl.BlockSpec((2,) + plane, lambda x: (0, x, 0, 0))
    return pl.pallas_call(
        last,
        grid=(LX // 2,),
        out_shape=[jax.ShapeDtypeStruct(field, F32), jax.ShapeDtypeStruct(field, F32), pair],
        in_specs=[pl.BlockSpec((4, 8, 128), lambda x: (0, 0, 0)), one, two, two],
        out_specs=[one, one, two],
    )(steps, right_side, kept, images)


def solution(mesh):
    placed = (
        P("row", "col", None), P("row", "col", None), P(), P(None, "row", None, None, "col"), P(), P(),
    )
    return jax.shard_map(
        local,
        mesh=mesh,
        in_specs=placed,
        out_specs=(P("row", "col", None), P("row", "col", None), P(None, "row", "col", None)),
        check_vma=False,
    )
```
